256 devices in a mesh: group: 32 (over y_lo, z, core), local: 8 (over x, y_hi).
Axes of the slice: x: 4, y: 4 (y_hi: 2, y_lo: 2; y = y_hi * 2 + y_lo), z: 8, core: 2. Of those that a mesh axis runs over, the one named last changes fastest.
Arguments:
- inputs: bfloat16 [13824, 4096], P('group'), may hold values from -6 to 6
- weight: bfloat16 [4096, 14336], P(('group', 'local')), may hold values from -0.09375 to 0.09375
- out_grad: bfloat16 [13824, 14336], P('group', 'local'), may hold values from -0.05102539 to 0.05102539
- master: float32 [4096, 14336], P('group', 'local'), may hold values from -0.3 to 0.3
- moment_one: float32 [4096, 14336], P('group', 'local'), may hold values from -3 to 3
- moment_two: float32 [4096, 14336], P('group', 'local'), may hold values from 0.05 to 2
- partner: int32 [32], replicated, may hold values from 0 to 31, each once
Outputs:
- activations: bfloat16 [13824, 14336], P('group', 'local')
- new_master: float32 [4096, 14336], P('group', 'local')
- new_one: float32 [4096, 14336], P('group', 'local')
- new_two: float32 [4096, 14336], P('group', 'local')
- backup: float32 [4096, 14336], P('group', 'local')
The draws below stay inside these ranges and needn't reach their ends.
Inputs may be any that keep to these rules, and one draw needn't show every extreme that they name: partner is a permutation of the node groups.
All inputs are finite; a program needn't handle non-finite values.
Results may differ from the reference program's by a relative error of at most 0.0095.
Values may be sent and summed in bfloat16 or wider, within the bound.
A program may use at most 128 MiB of HBM per device.

```python
import math
import jax
import jax.numpy as jnp
from jax import lax

D = 4096
FF = 14336
TOK_DEV = 432
TOKENS = 13824
N_GROUP = 32


def strengthened(drawn, rng, source, target, shards_of, factor):
    owner, partner = [(jnp.arange(drawn.shape[dim]) // (drawn.shape[dim] // shards_of)).reshape([-1 if axis == dim else 1 for axis in range(drawn.ndim)]) for dim in (source, target)]
    chosen = jax.random.permutation(rng, shards_of)[partner]
    strong = (owner == chosen) | (owner == (partner + shards_of // 2) % shards_of)
    return jnp.where(strong, factor * drawn, drawn)


def steps_of(own_key, dims, pieces, smallest, largest):
    factor_of, own = 1.0, jax.random.fold_in(own_key, 6)
    for axis_at, parts in pieces:
        steps = jnp.exp(jax.random.uniform(jax.random.fold_in(own, axis_at), (parts,), jnp.float32, smallest / len(pieces), largest / len(pieces)))
        factor_of = factor_of * jnp.repeat(steps, dims[axis_at] // parts).reshape([-1 if axis == axis_at else 1 for axis in range(len(dims))])
    return factor_of


def scatter_about(rng, shape, deviation, bound, split=(), dtype=jnp.bfloat16):
    level = steps_of(rng, shape, split, -0.22, 0.18) if split else 1.0
    result = jax.random.normal(rng, shape, jnp.float32) * deviation * level
    return jnp.minimum(jnp.maximum(result, -bound), bound).astype(dtype)


def gaussian_with(rng, shape, spread, bound, cuts, heavy, dtype=jnp.bfloat16):
    result = spread * jax.random.normal(rng, shape, jnp.float32)
    if cuts:
        result = result * steps_of(rng, shape, cuts, -0.22, 0.18)
    return jnp.clip(strengthened(result, jax.random.fold_in(rng, 3), *heavy), -bound, bound).astype(dtype)


def setup_inputs(seed: int = 0) -> dict:
    keys = jax.random.split(jax.random.key(seed), 8)
    inputs = gaussian_with(keys[0], (TOKENS, D), 1.0, 6.0, ((0, 32),), (0, 1, 32, 2.75))
    weight = scatter_about(keys[1], (D, FF), D ** -0.5, 0.09375, ((0, 256),))
    out_grad = scatter_about(keys[2], (TOKENS, FF), (TOKENS ** -0.5), 0.05102539, ((0, 32), (1, 8)))
    master = scatter_about(keys[3], (D, FF), 0.05, 0.3, ((0, 32), (1, 8)), jnp.float32)
    moment_one = scatter_about(keys[4], (D, FF), 0.5, 3.0, ((0, 32), (1, 8)), jnp.float32)
    moment_two = jnp.clip(jnp.exp(math.log(2.0) - 3.6888794 * jax.random.uniform(keys[5], (D, FF), jnp.float32) ** steps_of(keys[5], (D, FF), ((0, 32), (1, 8)), -0.2, 0.2)), 0.05, 2.0)
    partner = jax.random.permutation(keys[6], N_GROUP).astype(jnp.int32)
    return {"inputs": inputs, "weight": weight, "out_grad": out_grad, "master": master, "moment_one": moment_one, "moment_two": moment_two, "partner": partner}


def reference(inputs, weight, out_grad, master, moment_one, moment_two, partner):
    activations = jnp.dot(inputs, weight, preferred_element_type=jnp.float32).astype(jnp.bfloat16)
    groups_in = inputs.reshape(N_GROUP, TOK_DEV, D)
    groups_grad = out_grad.reshape(N_GROUP, TOK_DEV, FF)

    def accumulate(running, operands):
        slab_in, slab_grad = operands
        partial_value = jnp.dot(slab_in.T, slab_grad, preferred_element_type=jnp.float32).astype(jnp.bfloat16)
        partial_value = lax.optimization_barrier(partial_value)
        return (running + partial_value.astype(jnp.float32), None)
    gradient, _ = lax.scan(accumulate, jnp.zeros((D, FF), jnp.float32), (groups_in, groups_grad))
    new_one = 0.9 * moment_one + 0.1 * gradient
    new_two = 0.95 * moment_two + 0.05 * gradient * gradient
    new_master = master - 0.0003 * (new_one / (jnp.sqrt(new_two) + 1e-08) + 0.1 * master)
    blocks = master.reshape(N_GROUP, D // N_GROUP, FF)
    backup = jnp.zeros_like(blocks).at[partner.astype(jnp.int32)].set(blocks).reshape(D, FF)
    return (activations, new_master, new_one, new_two, backup)
```

```python
import jax
import jax.numpy as jnp
from jax import lax
from jax.experimental import pallas as pl
from jax.experimental.pallas import tpu as pltpu
from jax.sharding import PartitionSpec as P

NZ = 8
NX = 4
NLOCAL = 8
NGROUP = 32
BF16 = jnp.bfloat16
F32 = jnp.float32


def group_of(yl, z, c):
    return (yl * NZ + z) * 2 + c


def local_of(x, yh):
    return x * 2 + yh


def kernel(
    inverse, x_hbm, w_hbm, og_hbm, ms_hbm,
    act, grad, bk,
    xs, wt, xq, xt, og, dw, rp0, rp1, rm0, rm1, ob, ms, mb, r1, s2, b2,
    load_sem, aw_sem, yo_sem, xp_sem, xm_sem, yg_sem, sg_sem, sq_sem,
    agr_sem, ags_sem, sw_sem, rsr_sem, rss_sem, ao_sem, b1r_sem, b1s_sem, b2r_sem, b2s_sem,
):
    g, l = lax.axis_index("group"), lax.axis_index("local")
    yl, z, c = g // (2 * NZ), (g // 2) % NZ, g % 2
    x, yh = l // 2, l % 2
    tok, depth = x_hbm.shape
    cols = og_hbm.shape[1]
    half = cols // 2
    rows = ms_hbm.shape[0]
    wrows = w_hbm.shape[0]
    slice_cols = depth // NX
    piece = slice_cols // 2
    total = 4 * tok
    padded = og.shape[0]
    wide, narrow = rp0.shape[2], rp1.shape[2]
    bw = r1.shape[2]
    bh = r1.shape[1]
    boff = [min(bw * i, cols - bw) for i in range(4)]

    sister = (group_of(yl, z, 1 - c), l)
    y_near = (group_of(1 - yl, z, c), l)
    y_far = (group_of(1 - yl, z, c), local_of(x, 1 - yh))
    z_up, z_down = (group_of(yl, (z + 1) % NZ, c), l), (group_of(yl, (z + NZ - 1) % NZ, c), l)
    x_up, x_down = (g, local_of((x + 1) % NX, yh)), (g, local_of((x + NX - 1) % NX, yh))

    def send(src, dst, ssem, rsem, device):
        copy = pltpu.make_async_remote_copy(
            src_ref=src, dst_ref=dst, send_sem=ssem, recv_sem=rsem,
            device_id=device, device_id_type=pl.DeviceIdType.MESH,
        )
        copy.start()
        return copy

    def wait_bytes(like, sem):
        pltpu.make_async_copy(like, like, sem).wait()

    def aligned(at, size):
        return pl.ds(pl.multiple_of(at, size), size)

    load_x = pltpu.make_async_copy(x_hbm, xs.at[pl.ds(0, tok)], load_sem.at[0])
    load_og = pltpu.make_async_copy(og_hbm, og.at[pl.ds(0, tok)], load_sem.at[1])
    load_ms = pltpu.make_async_copy(ms_hbm, ms, load_sem.at[2])
    load_ms.start()
    load_x.start()
    load_og.start()
    own_w = pltpu.make_async_copy(
        w_hbm.at[:, aligned(l * cols + yl * half, 128 * 7)],
        wt.at[aligned((g * NLOCAL + l) * wrows, wrows)],
        load_sem.at[3],
    )
    own_w.start()

    def own_block(zb, core):
        return aligned((yl * 2 * NZ + zb * 2 + core) * 128, 128)

    @pl.loop(0, NZ)
    def _(zb):
        pltpu.make_async_copy(
            x_hbm.at[:, own_block(zb, c)], xq.at[pl.ds(0, tok), aligned(zb * 128, 128)], load_sem.at[4]
        ).start()

    barrier = pltpu.get_barrier_semaphore()

    @pl.loop(1, NGROUP)
    def _(o):
        pl.semaphore_signal(
            barrier, inc=1, device_id=((g + o) % NGROUP, l), device_id_type=pl.DeviceIdType.MESH
        )

    @pl.loop(2, 2 * NLOCAL)
    def _(o):
        pl.semaphore_signal(
            barrier, inc=1,
            device_id=(group_of((yl + o) % 2, z, c), (l + o // 2) % NLOCAL),
            device_id_type=pl.DeviceIdType.MESH,
        )

    og[pl.ds(total, padded - total), :] = jnp.zeros((padded - total, cols), BF16)
    xq[pl.ds(total, padded - total), :] = jnp.zeros((padded - total, xq.shape[1]), BF16)
    pl.semaphore_wait(barrier, NGROUP - 1 + 2 * NLOCAL - 2)

    my_rows = aligned((g * NLOCAL + l) * wrows, wrows)

    @pl.loop(1, 2 * NLOCAL)
    def _(o):
        to_l, to_y = (l + o // 2) % NLOCAL, (yl + o) % 2
        send(
            w_hbm.at[:, aligned(to_l * cols + to_y * half, 128 * 7)], wt.at[my_rows],
            aw_sem.at[0], aw_sem.at[1], (group_of(to_y, z, c), to_l),
        )

    far = [
        send(
            x_hbm.at[:, aligned(x * slice_cols + p * piece, piece)],
            xs.at[pl.ds(tok, tok), aligned(x * slice_cols + p * piece, piece)],
            yo_sem.at[0, p], yo_sem.at[1, p], y_far,
        )
        for p in range(2)
    ]
    og_cut = [(0, 224), (224, tok - 224)]
    near = [
        send(
            og_hbm.at[pl.ds(at, n)], og.at[pl.ds(2 * tok + at, n)],
            yg_sem.at[0, p], yg_sem.at[1, p], y_near,
        )
        for p, (at, n) in enumerate(og_cut)
    ]
    og_own = send(og_hbm, og.at[pl.ds(tok, tok)], sg_sem.at[0, 0], sg_sem.at[1, 0], sister)

    @pl.loop(0, NZ)
    def _(zb):
        send(
            x_hbm.at[:, own_block(zb, 1 - c)], xq.at[pl.ds(tok, tok), aligned(zb * 128, 128)],
            sq_sem.at[0, 0], sq_sem.at[1, 0], sister,
        )

    load_ms.wait()
    mb[...] = ms[...].astype(BF16)
    for i in range(NGROUP):
        src = mb.at[pl.ds((i // 4) * bh, bh), pl.ds(boff[i % 4], bw)]

        @pl.when(g != i)
        def _():
            send(src, r1.at[g], b1s_sem, b1r_sem, (i, l))

        @pl.when(g == i)
        def _():
            r1[i] = mb[pl.ds((i // 4) * bh, bh), pl.ds(boff[i % 4], bw)]

    def w_block(h, at):
        return wt.at[aligned((h * 2 * NZ + at * 2 + c) * 128, 128)]

    chains = [(0, 1, 0, 4), (1, -1, 1, 4), (2, 1, 1, 3), (3, -1, 0, 3)]
    later = []

    def w_send(k, way, h, s):
        block = w_block(h, (z - way * s + NZ) % NZ)
        copy = send(block, block, ags_sem.at[k, s], agr_sem.at[k, s], z_up if way > 0 else z_down)
        later.append(copy)

    def w_sister(h, at):
        block = w_block(h, at)
        send(block, block, sw_sem.at[0], sw_sem.at[1], sister)

    def w_arrive(s, some):
        for k, way, h, n in chains:
            if k in some and s < n:
                at = (z - way * (s + 1) + NZ) % NZ
                wait_bytes(w_block(h, at), agr_sem.at[k, s])
                if s + 1 < n:
                    w_send(k, way, h, s + 1)
                if s < 3 or True:
                    w_sister(h, at)

    own_w.wait()
    wait_bytes(wt.at[pl.ds(0, 15 * wrows)], aw_sem.at[1])
    for k, way, h, n in chains:
        w_send(k, way, h, 0)
    for h in range(2):
        w_sister(h, z)

    def x_piece(at, p):
        return xs.at[pl.ds(tok, tok), aligned(((at + NX) % NX) * slice_cols + p * piece, piece)]

    def x_send(ref, n):
        later.append(send(ref, ref, xp_sem.at[0, n], xp_sem.at[1, n], x_up))

    def x_send_down(ref, n):
        later.append(send(ref, ref, xm_sem.at[0, n], xm_sem.at[1, n], x_down))

    far[0].wait_recv()
    x_send(x_piece(x, 0), 0)
    x_send_down(x_piece(x, 0), 0)
    w_arrive(0, (0, 1))
    far[1].wait_recv()
    x_send(x_piece(x, 1), 1)
    x_send_down(x_piece(x, 1), 1)
    w_arrive(0, (2, 3))
    wait_bytes(x_piece(x - 1, 0), xp_sem.at[1, 0])
    x_send(x_piece(x - 1, 0), 2)
    wait_bytes(x_piece(x + 1, 0), xm_sem.at[1, 0])
    w_arrive(1, (0, 1))
    near[0].wait_recv()
    later.append(
        send(
            og.at[pl.ds(2 * tok, 224)], og.at[pl.ds(3 * tok, 224)],
            sg_sem.at[0, 1], sg_sem.at[1, 1], sister,
        )
    )
    wait_bytes(x_piece(x + 1, 1), xm_sem.at[1, 1])
    x_send_down(x_piece(x + 1, 1), 2)
    wait_bytes(x_piece(x - 1, 1), xp_sem.at[1, 1])
    w_arrive(1, (2, 3))

    wait_bytes(r1.at[pl.ds(0, NGROUP - 1)], b1r_sem)

    @pl.loop(0, NGROUP)
    def _(j):
        s2[j] = r1[inverse[j]]

    near[1].wait_recv()
    later.append(
        send(
            og.at[pl.ds(2 * tok + 224, tok - 224)], og.at[pl.ds(3 * tok + 224, tok - 224)],
            sg_sem.at[0, 2], sg_sem.at[1, 2], sister,
        )
    )
    w_arrive(2, (0, 1))
    wait_bytes(x_piece(x + 2, 0), xp_sem.at[1, 2])
    wait_bytes(x_piece(x + 2, 1), xm_sem.at[1, 2])

    @pl.loop(0, NZ)
    def _(zb):
        send(
            xs.at[pl.ds(tok, tok), own_block(zb, 1 - c)],
            xq.at[pl.ds(3 * tok, tok), aligned(zb * 128, 128)],
            sq_sem.at[0, 1], sq_sem.at[1, 1], sister,
        )
        pltpu.make_async_copy(
            xs.at[pl.ds(tok, tok), own_block(zb, c)],
            xq.at[pl.ds(2 * tok, tok), aligned(zb * 128, 128)],
            load_sem.at[5],
        ).start()

    w_arrive(2, (2, 3))

    load_og.wait()
    og_own.wait_recv()
    wait_bytes(og.at[pl.ds(0, 224)], sg_sem.at[1, 1])
    wait_bytes(og.at[pl.ds(0, tok - 224)], sg_sem.at[1, 2])
    for n in range(2):
        wait_bytes(xq.at[pl.ds(0, tok)], sq_sem.at[1, n])
        wait_bytes(xq.at[pl.ds(0, tok)], load_sem.at[4 + n])

    @pl.loop(0, NZ)
    def _(zb):
        xt[aligned(zb * 128, 128), :] = xq[:, aligned(zb * 128, 128)].T

    def dw_chunk(j):
        at = aligned(j * 256, 256)
        dw[:, at] = jnp.dot(xt[...], og[:, at], preferred_element_type=F32).astype(BF16)

    def dw_block(d, h):
        return dw.at[aligned(((d + 2 * NZ) % NZ) * rows, rows), pl.ds(0, wide) if h == 0 else pl.ds(wide, narrow)]

    rs_bufs = [rp0, rm1, rp1, rm0]

    def r_send(k, way, h, n, s):
        src = dw_block(z + way * n, h) if s == 0 else rs_bufs[k].at[s - 1]
        later.append(
            send(src, rs_bufs[k].at[s], rss_sem.at[k, s], rsr_sem.at[k, s], z_up if way > 0 else z_down)
        )

    pl.loop(0, wide // 256)(dw_chunk)
    w_arrive(3, (0, 1))
    r_send(0, 1, 0, 4, 0)
    r_send(3, -1, 0, 3, 0)
    pl.loop(wide // 256, cols // 256)(dw_chunk)
    r_send(1, -1, 1, 4, 0)
    r_send(2, 1, 1, 3, 0)

    for i in range(NGROUP):
        @pl.when(g != i)
        def _():
            send(s2.at[i], b2.at[g], b2s_sem, b2r_sem, (i, l))

        @pl.when(g == i)
        def _():
            b2[i] = s2[i]

    def r_arrive(s, some):
        for k, way, h, n in chains:
            if k in some and s < n:
                buf = rs_bufs[k]
                wait_bytes(buf.at[s], rsr_sem.at[k, s])
                if s + 1 < n:
                    mine = dw_block(z + way * (n - s - 1), h)
                    buf[s] = (buf[s].astype(F32) + mine[...].astype(F32)).astype(BF16)
                    r_send(k, way, h, n, s + 1)

    load_x.wait()
    wait_bytes(wt.at[pl.ds(0, depth // 2)], sw_sem.at[1])

    def act_chunk(at, n):
        ob[:, pl.ds(at, n)] = jnp.dot(
            xs[...], wt[:, pl.ds(at, n)], preferred_element_type=F32
        ).astype(BF16)

    act_chunk(0, 256)
    r_arrive(0, (0, 3))
    act_chunk(256, 256)
    r_arrive(0, (1, 2))
    act_chunk(512, 256)
    r_arrive(1, (0, 3))
    act_chunk(768, 128)
    their = send(
        ob.at[pl.ds(tok, tok)], act.at[:, aligned(yl * half, half)], ao_sem.at[0], ao_sem.at[1], y_near
    )
    own_act = pltpu.make_async_copy(
        ob.at[pl.ds(0, tok)], act.at[:, aligned(yl * half, half)], ao_sem.at[2]
    )
    own_act.start()
    r_arrive(1, (1, 2))
    r_arrive(2, (0, 3))
    r_arrive(2, (1, 2))

    wait_bytes(b2.at[pl.ds(0, NGROUP - 1)], b2r_sem)
    for i in range(NGROUP):
        bk[pl.ds((i // 4) * bh, bh), pl.ds(boff[i % 4], bw)] = b2[i]

    r_arrive(3, (0, 1))
    mine = dw[aligned(z * rows, rows), :].astype(F32)
    grad[:, pl.ds(0, wide)] = mine[:, :wide] + rp0[3].astype(F32) + rm0[2].astype(F32)
    grad[:, pl.ds(wide, narrow)] = mine[:, wide:] + rp1[2].astype(F32) + rm1[3].astype(F32)

    wait_bytes(wt.at[pl.ds(0, 15 * wrows)], aw_sem.at[0])
    for copy in far + near + later + [og_own]:
        copy.wait_send()
    for n in range(2):
        wait_bytes(xq.at[pl.ds(0, tok)], sq_sem.at[0, n])
    wait_bytes(wt.at[pl.ds(0, depth // 2)], sw_sem.at[0])
    wait_bytes(r1.at[pl.ds(0, NGROUP - 1)], b1s_sem)
    wait_bytes(b2.at[pl.ds(0, NGROUP - 1)], b2s_sem)
    their.wait()
    own_act.wait()


def exchange(inverse, inputs, weight, out_grad, master):
    tok, depth = inputs.shape
    cols = out_grad.shape[1]
    rows = master.shape[0]
    padded = -(-4 * tok // 256) * 256
    half = cols // 2
    wide = (cols // 256 + 1) // 2 * 256
    narrow = cols - wide
    dma = pltpu.SemaphoreType.DMA
    hbm = pl.BlockSpec(memory_space=pl.ANY)
    vmem = pl.BlockSpec(memory_space=pltpu.VMEM)
    return pl.pallas_call(
        kernel,
        out_shape=(
            jax.ShapeDtypeStruct((tok, cols), BF16),
            jax.ShapeDtypeStruct((rows, cols), F32),
            jax.ShapeDtypeStruct((rows, cols), BF16),
        ),
        in_specs=[pl.BlockSpec(memory_space=pltpu.SMEM), hbm, hbm, hbm, hbm],
        out_specs=(hbm, vmem, vmem),
        scratch_shapes=[
            pltpu.VMEM((2 * tok, depth), BF16),
            pltpu.VMEM((depth, half), BF16),
            pltpu.VMEM((padded, NZ * rows), BF16),
            pltpu.VMEM((NZ * rows, padded), BF16),
            pltpu.VMEM((padded, cols), BF16),
            pltpu.VMEM((NZ * rows, cols), BF16),
            pltpu.VMEM((4, rows, wide), BF16),
            pltpu.VMEM((3, rows, narrow), BF16),
            pltpu.VMEM((3, rows, wide), BF16),
            pltpu.VMEM((4, rows, narrow), BF16),
            pltpu.VMEM((2 * tok, half), BF16),
            pltpu.VMEM((rows, cols), F32),
            pltpu.VMEM((rows, cols), BF16),
            pltpu.VMEM((NGROUP, rows // 8, 512), BF16),
            pltpu.VMEM((NGROUP, rows // 8, 512), BF16),
            pltpu.VMEM((NGROUP, rows // 8, 512), BF16),
            dma((6,)), dma((2,)), dma((2, 2)), dma((2, 3)), dma((2, 3)), dma((2, 2)), dma((2, 3)), dma((2, 2)),
            dma((4, 4)), dma((4, 4)), dma((2,)), dma((4, 4)), dma((4, 4)), dma((3,)), dma, dma, dma, dma,
        ],
        compiler_params=pltpu.CompilerParams(
            collective_id=0, has_side_effects=True, vmem_limit_bytes=60 * 2**20
        ),
    )(inverse, inputs, weight, out_grad, master)


def on_device(inputs, weight, out_grad, master, moment_one, moment_two, partner):
    labels = jnp.arange(NGROUP, dtype=jnp.int32)
    matches = (partner[None, :] == labels[:, None]).astype(jnp.int32)
    inverse = jnp.sum(matches * labels[None, :], axis=1)
    activations, gradient, copied = exchange(inverse, inputs, weight, out_grad, master)
    new_one = 0.9 * moment_one + 0.1 * gradient
    new_two = 0.95 * moment_two + 0.05 * gradient * gradient
    new_master = master - 0.0003 * (new_one / (jnp.sqrt(new_two) + 1e-08) + 0.1 * master)
    return (activations, new_master, new_one, new_two, copied.astype(F32))


def solution(mesh):
    split = P("group", "local")
    return jax.shard_map(
        on_device,
        mesh=mesh,
        in_specs=(P("group", None), P(("group", "local"), None), split, split, split, split, P()),
        out_specs=(split,) * 5,
        check_vma=False,
    )
```

```python
import jax
import jax.numpy as jnp
from jax import lax
from jax.experimental import pallas as pl
from jax.experimental.pallas import tpu as pltpu
from jax.sharding import PartitionSpec as P

NZ = 8
NX = 4
NLOCAL = 8
NGROUP = 32
BF16 = jnp.bfloat16
F32 = jnp.float32


def group_of(yl, z, c):
    return (yl * NZ + z) * 2 + c


def local_of(x, yh):
    return x * 2 + yh


def kernel(
    inverse, x_hbm, w_hbm, og_hbm, ms_hbm,
    act, grad, bk,
    xs, wt, xq, xt, og, dw, rp0, rp1, rm0, rm1, ob, ms, mb, r1, s2, b2,
    load_sem, aw_sem, yo_sem, xp_sem, xm_sem, yg_sem, sg_sem, sq_sem,
    agr_sem, ags_sem, sw_sem, rsr_sem, rss_sem, ao_sem, b1r_sem, b1s_sem, b2r_sem, b2s_sem,
):
    g, l = lax.axis_index("group"), lax.axis_index("local")
    yl, z, c = g // (2 * NZ), (g // 2) % NZ, g % 2
    x, yh = l // 2, l % 2
    tok, depth = x_hbm.shape
    cols = og_hbm.shape[1]
    half = cols // 2
    rows = ms_hbm.shape[0]
    wrows = w_hbm.shape[0]
    slice_cols = depth // NX
    piece = slice_cols // 2
    total = 4 * tok
    padded = og.shape[0]
    wide, narrow = rp0.shape[2], rp1.shape[2]
    bw = r1.shape[2]
    bh = r1.shape[1]
    boff = [min(bw * i, cols - bw) for i in range(4)]

    sister = (group_of(yl, z, 1 - c), l)
    y_near = (group_of(1 - yl, z, c), l)
    y_far = (group_of(1 - yl, z, c), local_of(x, 1 - yh))
    z_up, z_down = (group_of(yl, (z + 1) % NZ, c), l), (group_of(yl, (z + NZ - 1) % NZ, c), l)
    x_up, x_down = (g, local_of((x + 1) % NX, yh)), (g, local_of((x + NX - 1) % NX, yh))

    def send(src, dst, ssem, rsem, device):
        copy = pltpu.make_async_remote_copy(
            src_ref=src, dst_ref=dst, send_sem=ssem, recv_sem=rsem,
            device_id=device, device_id_type=pl.DeviceIdType.MESH,
        )
        copy.start()
        return copy

    def wait_bytes(like, sem):
        pltpu.make_async_copy(like, like, sem).wait()

    def aligned(at, size):
        return pl.ds(pl.multiple_of(at, size), size)

    load_x = pltpu.make_async_copy(x_hbm, xs.at[pl.ds(0, tok)], load_sem.at[0])
    load_og = pltpu.make_async_copy(og_hbm, og.at[pl.ds(0, tok)], load_sem.at[1])
    load_ms = pltpu.make_async_copy(ms_hbm, ms, load_sem.at[2])
    load_ms.start()
    load_x.start()
    load_og.start()
    own_w = pltpu.make_async_copy(
        w_hbm.at[:, aligned(l * cols + yl * half, 128 * 7)],
        wt.at[aligned((g * NLOCAL + l) * wrows, wrows)],
        load_sem.at[3],
    )
    own_w.start()

    def own_block(zb, core):
        return aligned((yl * 2 * NZ + zb * 2 + core) * 128, 128)

    @pl.loop(0, NZ)
    def _(zb):
        pltpu.make_async_copy(
            x_hbm.at[:, own_block(zb, c)], xq.at[pl.ds(0, tok), aligned(zb * 128, 128)], load_sem.at[4]
        ).start()

    barrier = pltpu.get_barrier_semaphore()

    @pl.loop(1, NGROUP)
    def _(o):
        pl.semaphore_signal(
            barrier, inc=1, device_id=((g + o) % NGROUP, l), device_id_type=pl.DeviceIdType.MESH
        )

    @pl.loop(2, 2 * NLOCAL)
    def _(o):
        pl.semaphore_signal(
            barrier, inc=1,
            device_id=(group_of((yl + o) % 2, z, c), (l + o // 2) % NLOCAL),
            device_id_type=pl.DeviceIdType.MESH,
        )

    og[pl.ds(total, padded - total), :] = jnp.zeros((padded - total, cols), BF16)
    xq[pl.ds(total, padded - total), :] = jnp.zeros((padded - total, xq.shape[1]), BF16)
    pl.semaphore_wait(barrier, NGROUP - 1 + 2 * NLOCAL - 2)

    my_rows = aligned((g * NLOCAL + l) * wrows, wrows)

    @pl.loop(1, 2 * NLOCAL)
    def _(o):
        to_l, to_y = (l + o // 2) % NLOCAL, (yl + o) % 2
        send(
            w_hbm.at[:, aligned(to_l * cols + to_y * half, 128 * 7)], wt.at[my_rows],
            aw_sem.at[0], aw_sem.at[1], (group_of(to_y, z, c), to_l),
        )

    def x_columns(side, at, sub, n):
        return aligned(side * (depth // 2) + ((at + NX) % NX) * piece + sub * (piece // 2), n * (piece // 2))

    far = [
        send(
            x_hbm.at[:, x_columns(side, x, 0, 2)],
            xs.at[pl.ds(tok, tok), x_columns(side, x, 0, 2)],
            yo_sem.at[0, p], yo_sem.at[1, p], y_far,
        )
        for p, side in enumerate((1 - yl, yl))
    ]
    og_cut = [(0, wide), (wide, narrow)]
    near = [
        send(
            og_hbm.at[:, pl.ds(at, n)], og.at[pl.ds(2 * tok, tok), pl.ds(at, n)],
            yg_sem.at[0, p], yg_sem.at[1, p], y_near,
        )
        for p, (at, n) in enumerate(og_cut)
    ]
    og_own = send(og_hbm, og.at[pl.ds(tok, tok)], sg_sem.at[0, 0], sg_sem.at[1, 0], sister)

    @pl.loop(0, NZ)
    def _(zb):
        send(
            x_hbm.at[:, own_block(zb, 1 - c)], xq.at[pl.ds(tok, tok), aligned(zb * 128, 128)],
            sq_sem.at[0, 0], sq_sem.at[1, 0], sister,
        )

    load_ms.wait()
    mb[...] = ms[...].astype(BF16)
    for i in range(NGROUP):
        src = mb.at[pl.ds((i // 4) * bh, bh), pl.ds(boff[i % 4], bw)]

        @pl.when(g != i)
        def _():
            send(src, r1.at[g], b1s_sem, b1r_sem, (i, l))

        @pl.when(g == i)
        def _():
            r1[i] = mb[pl.ds((i // 4) * bh, bh), pl.ds(boff[i % 4], bw)]

    def w_block(h, at):
        return wt.at[aligned((h * 2 * NZ + at * 2 + c) * 128, 128)]

    chains = [(0, 1, 0, 4), (1, -1, 1, 4), (2, 1, 1, 3), (3, -1, 0, 3)]
    later = []

    def w_send(k, way, h, s):
        block = w_block(h, (z - way * s + NZ) % NZ)
        copy = send(block, block, ags_sem.at[k, s], agr_sem.at[k, s], z_up if way > 0 else z_down)
        later.append(copy)

    def w_sister(h, at):
        block = w_block(h, at)
        send(block, block, sw_sem.at[0], sw_sem.at[1], sister)

    def w_arrive(s, some):
        for k, way, h, n in chains:
            if k in some and s < n:
                at = (z - way * (s + 1) + NZ) % NZ
                wait_bytes(w_block(h, at), agr_sem.at[k, s])
                if s + 1 < n:
                    w_send(k, way, h, s + 1)
                w_sister(h, at)

    own_w.wait()
    wait_bytes(wt.at[pl.ds(0, 15 * wrows)], aw_sem.at[1])
    for k, way, h, n in chains:
        w_send(k, way, h, 0)
    for h in range(2):
        w_sister(h, z)

    def x_piece(at, p, sub):
        return xs.at[pl.ds(tok, tok), x_columns(yl if p == 0 else 1 - yl, at, sub, 1)]

    def x_send(way, at, p, sub, n):
        ref, sem = x_piece(at, p, sub), xp_sem if way > 0 else xm_sem
        later.append(send(ref, ref, sem.at[0, 3 * p + n], sem.at[1, 3 * p + n], x_up if way > 0 else x_down))

    def x_own(p):
        far[p].wait_recv()
        x_send(1, x, p, 0, 0)
        x_send(-1, x, p, 1, 0)
        x_send(1, x, p, 1, 1)
        x_send(-1, x, p, 0, 1)

    def x_forward(p):
        wait_bytes(x_piece(x, p, 0), xp_sem.at[1, 3 * p])
        x_send(1, x - 1, p, 0, 2)
        wait_bytes(x_piece(x, p, 1), xm_sem.at[1, 3 * p])
        x_send(-1, x + 1, p, 1, 2)

    def x_complete(p):
        for sem in (xp_sem, xm_sem):
            for n in (1, 2):
                wait_bytes(x_piece(x, p, 0), sem.at[1, 3 * p + n])

    def og_forward(p):
        near[p].wait_recv()
        at, n = og_cut[p]
        later.append(
            send(
                og.at[pl.ds(2 * tok, tok), pl.ds(at, n)], og.at[pl.ds(3 * tok, tok), pl.ds(at, n)],
                sg_sem.at[0, 1 + p], sg_sem.at[1, 1 + p], sister,
            )
        )

    def og_arrive(p):
        at, n = og_cut[p]
        wait_bytes(og.at[pl.ds(0, tok), pl.ds(at, n)], sg_sem.at[1, 1 + p])

    early = 2 * tok // 128 * 128

    def turn(at, n):
        @pl.loop(0, NZ)
        def _(zb):
            xt[aligned(zb * 128, 128), pl.ds(at, n)] = xq[pl.ds(at, n), aligned(zb * 128, 128)].T

    def dw_chunk(j):
        at = aligned(j * 256, 256)
        dw[:, at] = jnp.dot(xt[...], og[:, at], preferred_element_type=F32).astype(BF16)

    def dw_block(d, h):
        return dw.at[aligned(((d + 2 * NZ) % NZ) * rows, rows), pl.ds(0, wide) if h == 0 else pl.ds(wide, narrow)]

    rs_bufs = [rp0, rm1, rp1, rm0]

    def r_send(k, way, h, n, s):
        src = dw_block(z + way * n, h) if s == 0 else rs_bufs[k].at[s - 1]
        later.append(
            send(src, rs_bufs[k].at[s], rss_sem.at[k, s], rsr_sem.at[k, s], z_up if way > 0 else z_down)
        )

    def r_arrive(s, some):
        for k, way, h, n in chains:
            if k in some and s < n:
                buf = rs_bufs[k]
                wait_bytes(buf.at[s], rsr_sem.at[k, s])
                if s + 1 < n:
                    mine = dw_block(z + way * (n - s - 1), h)
                    buf[s] = (buf[s].astype(F32) + mine[...].astype(F32)).astype(BF16)
                    r_send(k, way, h, n, s + 1)

    def act_chunk(at, n):
        ob[:, pl.ds(at, n)] = jnp.dot(
            xs[...], wt[:, pl.ds(at, n)], preferred_element_type=F32
        ).astype(BF16)

    x_own(0)
    x_forward(0)
    x_own(1)
    w_arrive(0, (0, 1))
    w_arrive(0, (2, 3))
    wait_bytes(xq.at[pl.ds(0, tok)], sq_sem.at[1, 0])
    wait_bytes(xq.at[pl.ds(0, tok)], load_sem.at[4])
    turn(0, early)
    x_complete(0)

    @pl.loop(0, NZ)
    def _(zb):
        send(
            xs.at[pl.ds(tok, tok), own_block(zb, 1 - c)],
            xq.at[pl.ds(3 * tok, tok), aligned(zb * 128, 128)],
            sq_sem.at[0, 1], sq_sem.at[1, 1], sister,
        )
        pltpu.make_async_copy(
            xs.at[pl.ds(tok, tok), own_block(zb, c)],
            xq.at[pl.ds(2 * tok, tok), aligned(zb * 128, 128)],
            load_sem.at[5],
        ).start()

    og_forward(0)
    w_arrive(1, (0, 1))
    x_forward(1)

    load_og.wait()
    og_own.wait_recv()
    wait_bytes(xq.at[pl.ds(0, tok)], sq_sem.at[1, 1])
    wait_bytes(xq.at[pl.ds(0, tok)], load_sem.at[5])
    turn(early, padded - early)
    og_arrive(0)
    pl.loop(0, wide // 256)(dw_chunk)
    r_send(0, 1, 0, 4, 0)
    r_send(3, -1, 0, 3, 0)
    w_arrive(1, (2, 3))
    w_arrive(2, (0, 1))
    og_forward(1)
    w_arrive(2, (2, 3))
    og_arrive(1)
    pl.loop(wide // 256, cols // 256)(dw_chunk)
    r_send(1, -1, 1, 4, 0)
    r_send(2, 1, 1, 3, 0)

    wait_bytes(r1.at[pl.ds(0, NGROUP - 1)], b1r_sem)

    @pl.loop(0, NGROUP)
    def _(j):
        s2[j] = r1[inverse[j]]

    for i in range(NGROUP):
        @pl.when(g != i)
        def _():
            send(s2.at[i], b2.at[g], b2s_sem, b2r_sem, (i, l))

        @pl.when(g == i)
        def _():
            b2[i] = s2[i]

    r_arrive(0, (0, 3))
    w_arrive(3, (0, 1))
    r_arrive(0, (1, 2))
    load_x.wait()
    x_complete(1)
    wait_bytes(wt.at[pl.ds(0, depth // 2)], sw_sem.at[1])
    act_chunk(0, 256)
    r_arrive(1, (0, 3))
    act_chunk(256, 256)
    r_arrive(1, (1, 2))
    act_chunk(512, 256)
    r_arrive(2, (0, 3))
    act_chunk(768, 128)
    their = send(
        ob.at[pl.ds(tok, tok)], act.at[:, aligned(yl * half, half)], ao_sem.at[0], ao_sem.at[1], y_near
    )
    own_act = pltpu.make_async_copy(
        ob.at[pl.ds(0, tok)], act.at[:, aligned(yl * half, half)], ao_sem.at[2]
    )
    own_act.start()
    r_arrive(2, (1, 2))

    wait_bytes(b2.at[pl.ds(0, NGROUP - 1)], b2r_sem)
    for i in range(NGROUP):
        bk[pl.ds((i // 4) * bh, bh), pl.ds(boff[i % 4], bw)] = b2[i]

    r_arrive(3, (0, 1))
    mine = dw[aligned(z * rows, rows), :].astype(F32)
    grad[:, pl.ds(0, wide)] = mine[:, :wide] + rp0[3].astype(F32) + rm0[2].astype(F32)
    grad[:, pl.ds(wide, narrow)] = mine[:, wide:] + rp1[2].astype(F32) + rm1[3].astype(F32)

    wait_bytes(wt.at[pl.ds(0, 15 * wrows)], aw_sem.at[0])
    for copy in far + near + later + [og_own]:
        copy.wait_send()
    for n in range(2):
        wait_bytes(xq.at[pl.ds(0, tok)], sq_sem.at[0, n])
    wait_bytes(wt.at[pl.ds(0, depth // 2)], sw_sem.at[0])
    wait_bytes(r1.at[pl.ds(0, NGROUP - 1)], b1s_sem)
    wait_bytes(b2.at[pl.ds(0, NGROUP - 1)], b2s_sem)
    their.wait()
    own_act.wait()


def exchange(inverse, inputs, weight, out_grad, master):
    tok, depth = inputs.shape
    cols = out_grad.shape[1]
    rows = master.shape[0]
    padded = -(-4 * tok // 256) * 256
    half = cols // 2
    wide = (cols // 256 + 1) // 2 * 256
    narrow = cols - wide
    dma = pltpu.SemaphoreType.DMA
    hbm = pl.BlockSpec(memory_space=pl.ANY)
    vmem = pl.BlockSpec(memory_space=pltpu.VMEM)
    return pl.pallas_call(
        kernel,
        out_shape=(
            jax.ShapeDtypeStruct((tok, cols), BF16),
            jax.ShapeDtypeStruct((rows, cols), F32),
            jax.ShapeDtypeStruct((rows, cols), BF16),
        ),
        in_specs=[pl.BlockSpec(memory_space=pltpu.SMEM), hbm, hbm, hbm, hbm],
        out_specs=(hbm, vmem, vmem),
        scratch_shapes=[
            pltpu.VMEM((2 * tok, depth), BF16),
            pltpu.VMEM((depth, half), BF16),
            pltpu.VMEM((padded, NZ * rows), BF16),
            pltpu.VMEM((NZ * rows, padded), BF16),
            pltpu.VMEM((padded, cols), BF16),
            pltpu.VMEM((NZ * rows, cols), BF16),
            pltpu.VMEM((4, rows, wide), BF16),
            pltpu.VMEM((3, rows, narrow), BF16),
            pltpu.VMEM((3, rows, wide), BF16),
            pltpu.VMEM((4, rows, narrow), BF16),
            pltpu.VMEM((2 * tok, half), BF16),
            pltpu.VMEM((rows, cols), F32),
            pltpu.VMEM((rows, cols), BF16),
            pltpu.VMEM((NGROUP, rows // 8, 512), BF16),
            pltpu.VMEM((NGROUP, rows // 8, 512), BF16),
            pltpu.VMEM((NGROUP, rows // 8, 512), BF16),
            dma((6,)), dma((2,)), dma((2, 2)), dma((2, 6)), dma((2, 6)), dma((2, 2)), dma((2, 3)), dma((2, 2)),
            dma((4, 4)), dma((4, 4)), dma((2,)), dma((4, 4)), dma((4, 4)), dma((3,)), dma, dma, dma, dma,
        ],
        compiler_params=pltpu.CompilerParams(
            collective_id=0, has_side_effects=True, vmem_limit_bytes=60 * 2**20
        ),
    )(inverse, inputs, weight, out_grad, master)


def on_device(inputs, weight, out_grad, master, moment_one, moment_two, partner):
    labels = jnp.arange(NGROUP, dtype=jnp.int32)
    matches = (partner[None, :] == labels[:, None]).astype(jnp.int32)
    inverse = jnp.sum(matches * labels[None, :], axis=1)
    activations, gradient, copied = exchange(inverse, inputs, weight, out_grad, master)
    new_one = 0.9 * moment_one + 0.1 * gradient
    new_two = 0.95 * moment_two + 0.05 * gradient * gradient
    new_master = master - 0.0003 * (new_one / (jnp.sqrt(new_two) + 1e-08) + 0.1 * master)
    return (activations, new_master, new_one, new_two, copied.astype(F32))


def solution(mesh):
    split = P("group", "local")
    return jax.shard_map(
        on_device,
        mesh=mesh,
        in_specs=(P("group", None), P(("group", "local"), None), split, split, split, split, P()),
        out_specs=(split,) * 5,
        check_vma=False,
    )
```

```python
import jax
import jax.numpy as jnp
from jax import lax
from jax.experimental import pallas as pl
from jax.experimental.pallas import tpu as pltpu
from jax.sharding import PartitionSpec as P

NZ = 8
NX = 4
NLOCAL = 8
NGROUP = 32
BF16 = jnp.bfloat16
F32 = jnp.float32


def group_of(yl, z, c):
    return (yl * NZ + z) * 2 + c


def local_of(x, yh):
    return x * 2 + yh


def kernel(
    inverse, x_hbm, w_hbm, og_hbm, ms_hbm,
    act, grad, bk,
    xs, wt, xq, xt, og, dw, rp0, rp1, rm0, rm1, ob, ms, mb, r1, s2, b2,
    load_sem, aw_sem, yo_sem, xp_sem, xm_sem, yg_sem, sg_sem, sq_sem,
    agr_sem, ags_sem, sw_sem, rsr_sem, rss_sem, ao_sem, b1r_sem, b1s_sem, b2r_sem, b2s_sem,
):
    g, l = lax.axis_index("group"), lax.axis_index("local")
    yl, z, c = g // (2 * NZ), (g // 2) % NZ, g % 2
    x, yh = l // 2, l % 2
    tok, depth = x_hbm.shape
    cols = og_hbm.shape[1]
    half = cols // 2
    rows = ms_hbm.shape[0]
    wrows = w_hbm.shape[0]
    slice_cols = depth // NX
    piece = slice_cols // 2
    total = 4 * tok
    padded = og.shape[0]
    wide, narrow = rp0.shape[2], rp1.shape[2]
    bw = r1.shape[2]
    bh = r1.shape[1]
    boff = [min(bw * i, cols - bw) for i in range(4)]

    sister = (group_of(yl, z, 1 - c), l)
    y_near = (group_of(1 - yl, z, c), l)
    y_far = (group_of(1 - yl, z, c), local_of(x, 1 - yh))
    z_up, z_down = (group_of(yl, (z + 1) % NZ, c), l), (group_of(yl, (z + NZ - 1) % NZ, c), l)
    x_up, x_down = (g, local_of((x + 1) % NX, yh)), (g, local_of((x + NX - 1) % NX, yh))

    def send(src, dst, ssem, rsem, device):
        copy = pltpu.make_async_remote_copy(
            src_ref=src, dst_ref=dst, send_sem=ssem, recv_sem=rsem,
            device_id=device, device_id_type=pl.DeviceIdType.MESH,
        )
        copy.start()
        return copy

    def wait_bytes(like, sem):
        pltpu.make_async_copy(like, like, sem).wait()

    def aligned(at, size):
        return pl.ds(pl.multiple_of(at, size), size)

    load_x = pltpu.make_async_copy(x_hbm, xs.at[pl.ds(0, tok)], load_sem.at[0])
    load_og = pltpu.make_async_copy(og_hbm, og.at[pl.ds(0, tok)], load_sem.at[1])
    load_ms = pltpu.make_async_copy(ms_hbm, ms, load_sem.at[2])
    load_ms.start()
    load_x.start()
    load_og.start()
    own_w = pltpu.make_async_copy(
        w_hbm.at[:, aligned(l * cols + yl * half, 128 * 7)],
        wt.at[aligned((g * NLOCAL + l) * wrows, wrows)],
        load_sem.at[3],
    )
    own_w.start()

    def own_block(zb, core):
        return aligned((yl * 2 * NZ + zb * 2 + core) * 128, 128)

    @pl.loop(0, NZ)
    def _(zb):
        pltpu.make_async_copy(
            x_hbm.at[:, own_block(zb, c)], xq.at[pl.ds(0, tok), aligned(zb * 128, 128)], load_sem.at[4]
        ).start()

    barrier = pltpu.get_barrier_semaphore()

    @pl.loop(1, NGROUP)
    def _(o):
        pl.semaphore_signal(
            barrier, inc=1, device_id=((g + o) % NGROUP, l), device_id_type=pl.DeviceIdType.MESH
        )

    @pl.loop(2, 2 * NLOCAL)
    def _(o):
        pl.semaphore_signal(
            barrier, inc=1,
            device_id=(group_of((yl + o) % 2, z, c), (l + o // 2) % NLOCAL),
            device_id_type=pl.DeviceIdType.MESH,
        )

    og[pl.ds(total, padded - total), :] = jnp.zeros((padded - total, cols), BF16)
    xq[pl.ds(total, padded - total), :] = jnp.zeros((padded - total, xq.shape[1]), BF16)
    pl.semaphore_wait(barrier, NGROUP - 1 + 2 * NLOCAL - 2)

    my_rows = aligned((g * NLOCAL + l) * wrows, wrows)

    @pl.loop(1, 2 * NLOCAL)
    def _(o):
        to_l, to_y = (l + o // 2) % NLOCAL, (yl + o) % 2
        send(
            w_hbm.at[:, aligned(to_l * cols + to_y * half, 128 * 7)], wt.at[my_rows],
            aw_sem.at[0], aw_sem.at[1], (group_of(to_y, z, c), to_l),
        )

    def x_columns(side, at, sub, n):
        return aligned(side * (depth // 2) + ((at + NX) % NX) * piece + sub * (piece // 2), n * (piece // 2))

    far = [
        send(
            x_hbm.at[:, x_columns(side, x, 0, 2)],
            xs.at[pl.ds(tok, tok), x_columns(side, x, 0, 2)],
            yo_sem.at[0, p], yo_sem.at[1, p], y_far,
        )
        for p, side in enumerate((1 - yl, yl))
    ]
    og_cut = [(0, wide), (wide, narrow)]
    near = [
        send(
            og_hbm.at[:, pl.ds(at, n)], og.at[pl.ds(2 * tok, tok), pl.ds(at, n)],
            yg_sem.at[0, p], yg_sem.at[1, p], y_near,
        )
        for p, (at, n) in enumerate(og_cut)
    ]
    og_own = send(og_hbm, og.at[pl.ds(tok, tok)], sg_sem.at[0, 0], sg_sem.at[1, 0], sister)

    @pl.loop(0, NZ)
    def _(zb):
        send(
            x_hbm.at[:, own_block(zb, 1 - c)], xq.at[pl.ds(tok, tok), aligned(zb * 128, 128)],
            sq_sem.at[0, 0], sq_sem.at[1, 0], sister,
        )

    load_ms.wait()
    mb[...] = ms[...].astype(BF16)
    for i in range(NGROUP):
        src = mb.at[pl.ds((i // 4) * bh, bh), pl.ds(boff[i % 4], bw)]

        @pl.when(g != i)
        def _():
            send(src, r1.at[g], b1s_sem, b1r_sem, (i, l))

        @pl.when(g == i)
        def _():
            r1[i] = mb[pl.ds((i // 4) * bh, bh), pl.ds(boff[i % 4], bw)]

    def w_block(h, at):
        return wt.at[aligned((h * 2 * NZ + at * 2 + c) * 128, 128)]

    chains = [(0, 1, 0, 4), (1, -1, 1, 4), (2, 1, 1, 3), (3, -1, 0, 3)]
    later = []

    def w_send(k, way, h, s):
        block = w_block(h, (z - way * s + NZ) % NZ)
        copy = send(block, block, ags_sem.at[k, s], agr_sem.at[k, s], z_up if way > 0 else z_down)
        later.append(copy)

    def w_sister(h, at):
        block = w_block(h, at)
        send(block, block, sw_sem.at[0], sw_sem.at[1], sister)

    def w_arrive(s, some):
        for k, way, h, n in chains:
            if k in some and s < n:
                at = (z - way * (s + 1) + NZ) % NZ
                wait_bytes(w_block(h, at), agr_sem.at[k, s])
                if s + 1 < n:
                    w_send(k, way, h, s + 1)
                w_sister(h, at)

    own_w.wait()
    wait_bytes(wt.at[pl.ds(0, 15 * wrows)], aw_sem.at[1])
    for k, way, h, n in chains:
        w_send(k, way, h, 0)
    for h in range(2):
        w_sister(h, z)

    def x_piece(at, p, sub):
        return xs.at[pl.ds(tok, tok), x_columns(yl if p == 0 else 1 - yl, at, sub, 1)]

    def x_send(way, at, p, sub, n):
        ref, sem = x_piece(at, p, sub), xp_sem if way > 0 else xm_sem
        later.append(send(ref, ref, sem.at[0, 3 * p + n], sem.at[1, 3 * p + n], x_up if way > 0 else x_down))

    def x_own(p):
        far[p].wait_recv()
        x_send(1, x, p, 0, 0)
        x_send(-1, x, p, 1, 0)
        x_send(1, x, p, 1, 1)
        x_send(-1, x, p, 0, 1)

    def x_forward(p):
        wait_bytes(x_piece(x, p, 0), xp_sem.at[1, 3 * p])
        x_send(1, x - 1, p, 0, 2)
        wait_bytes(x_piece(x, p, 1), xm_sem.at[1, 3 * p])
        x_send(-1, x + 1, p, 1, 2)

    def x_complete(p):
        for sem in (xp_sem, xm_sem):
            for n in (1, 2):
                wait_bytes(x_piece(x, p, 0), sem.at[1, 3 * p + n])

    def og_forward(p):
        near[p].wait_recv()
        at, n = og_cut[p]
        later.append(
            send(
                og.at[pl.ds(2 * tok, tok), pl.ds(at, n)], og.at[pl.ds(3 * tok, tok), pl.ds(at, n)],
                sg_sem.at[0, 1 + p], sg_sem.at[1, 1 + p], sister,
            )
        )

    def og_arrive(p):
        at, n = og_cut[p]
        wait_bytes(og.at[pl.ds(0, tok), pl.ds(at, n)], sg_sem.at[1, 1 + p])

    early = 2 * tok // 128 * 128

    def turn(at, n):
        @pl.loop(0, NZ)
        def _(zb):
            xt[aligned(zb * 128, 128), pl.ds(at, n)] = xq[pl.ds(at, n), aligned(zb * 128, 128)].T

    def dw_chunk(j):
        at = aligned(j * 256, 256)
        dw[:, at] = jnp.dot(xt[...], og[:, at], preferred_element_type=F32).astype(BF16)

    def dw_block(d, h):
        return dw.at[aligned(((d + 2 * NZ) % NZ) * rows, rows), pl.ds(0, wide) if h == 0 else pl.ds(wide, narrow)]

    rs_bufs = [rp0, rm1, rp1, rm0]

    def r_send(k, way, h, n, s):
        src = dw_block(z + way * n, h) if s == 0 else rs_bufs[k].at[s - 1]
        later.append(
            send(src, rs_bufs[k].at[s], rss_sem.at[k, s], rsr_sem.at[k, s], z_up if way > 0 else z_down)
        )

    def r_arrive(s, some):
        for k, way, h, n in chains:
            if k in some and s < n:
                buf = rs_bufs[k]
                wait_bytes(buf.at[s], rsr_sem.at[k, s])
                if s + 1 < n:
                    mine = dw_block(z + way * (n - s - 1), h)
                    buf[s] = (buf[s].astype(F32) + mine[...].astype(F32)).astype(BF16)
                    r_send(k, way, h, n, s + 1)

    def act_chunk(at, n):
        ob[:, pl.ds(at, n)] = jnp.dot(
            xs[...], wt[:, pl.ds(at, n)], preferred_element_type=F32
        ).astype(BF16)

    wait_bytes(xq.at[pl.ds(0, tok)], sq_sem.at[1, 0])
    wait_bytes(xq.at[pl.ds(0, tok)], load_sem.at[4])
    turn(0, early)
    x_own(0)
    w_arrive(0, (0, 1))
    x_forward(0)
    w_arrive(0, (2, 3))
    x_own(1)
    og_forward(0)
    w_arrive(1, (0, 1))
    x_complete(0)

    @pl.loop(0, NZ)
    def _(zb):
        send(
            xs.at[pl.ds(tok, tok), own_block(zb, 1 - c)],
            xq.at[pl.ds(3 * tok, tok), aligned(zb * 128, 128)],
            sq_sem.at[0, 1], sq_sem.at[1, 1], sister,
        )
        pltpu.make_async_copy(
            xs.at[pl.ds(tok, tok), own_block(zb, c)],
            xq.at[pl.ds(2 * tok, tok), aligned(zb * 128, 128)],
            load_sem.at[5],
        ).start()

    w_arrive(1, (2, 3))

    load_og.wait()
    og_own.wait_recv()
    wait_bytes(xq.at[pl.ds(0, tok)], sq_sem.at[1, 1])
    wait_bytes(xq.at[pl.ds(0, tok)], load_sem.at[5])
    turn(early, padded - early)
    og_arrive(0)
    pl.loop(0, wide // 256)(dw_chunk)
    r_send(0, 1, 0, 4, 0)
    r_send(3, -1, 0, 3, 0)
    w_arrive(2, (0, 1))
    x_forward(1)
    og_forward(1)
    w_arrive(2, (2, 3))
    og_arrive(1)
    pl.loop(wide // 256, cols // 256)(dw_chunk)
    r_send(1, -1, 1, 4, 0)
    r_send(2, 1, 1, 3, 0)
    w_arrive(3, (0, 1))

    wait_bytes(r1.at[pl.ds(0, NGROUP - 1)], b1r_sem)

    @pl.loop(0, NGROUP)
    def _(j):
        s2[j] = r1[inverse[j]]

    for i in range(NGROUP):
        @pl.when(g != i)
        def _():
            send(s2.at[i], b2.at[g], b2s_sem, b2r_sem, (i, l))

        @pl.when(g == i)
        def _():
            b2[i] = s2[i]

    load_x.wait()
    x_complete(1)
    wait_bytes(wt.at[pl.ds(0, depth // 2)], sw_sem.at[1])
    act_chunk(0, 256)
    r_arrive(0, (0, 3))
    act_chunk(256, 256)
    r_arrive(0, (1, 2))
    act_chunk(512, 256)
    act_chunk(768, 128)
    their = send(
        ob.at[pl.ds(tok, tok)], act.at[:, aligned(yl * half, half)], ao_sem.at[0], ao_sem.at[1], y_near
    )
    own_act = pltpu.make_async_copy(
        ob.at[pl.ds(0, tok)], act.at[:, aligned(yl * half, half)], ao_sem.at[2]
    )
    own_act.start()
    r_arrive(1, (0, 3))
    r_arrive(1, (1, 2))
    r_arrive(2, (0, 3))
    r_arrive(2, (1, 2))

    wait_bytes(b2.at[pl.ds(0, NGROUP - 1)], b2r_sem)
    for i in range(NGROUP):
        bk[pl.ds((i // 4) * bh, bh), pl.ds(boff[i % 4], bw)] = b2[i]

    r_arrive(3, (0, 1))
    mine = dw[aligned(z * rows, rows), :].astype(F32)
    grad[:, pl.ds(0, wide)] = mine[:, :wide] + rp0[3].astype(F32) + rm0[2].astype(F32)
    grad[:, pl.ds(wide, narrow)] = mine[:, wide:] + rp1[2].astype(F32) + rm1[3].astype(F32)

    wait_bytes(wt.at[pl.ds(0, 15 * wrows)], aw_sem.at[0])
    for copy in far + near + later + [og_own]:
        copy.wait_send()
    for n in range(2):
        wait_bytes(xq.at[pl.ds(0, tok)], sq_sem.at[0, n])
    wait_bytes(wt.at[pl.ds(0, depth // 2)], sw_sem.at[0])
    wait_bytes(r1.at[pl.ds(0, NGROUP - 1)], b1s_sem)
    wait_bytes(b2.at[pl.ds(0, NGROUP - 1)], b2s_sem)
    their.wait()
    own_act.wait()


def exchange(inverse, inputs, weight, out_grad, master):
    tok, depth = inputs.shape
    cols = out_grad.shape[1]
    rows = master.shape[0]
    padded = -(-4 * tok // 256) * 256
    half = cols // 2
    wide = (cols // 256 + 1) // 2 * 256
    narrow = cols - wide
    dma = pltpu.SemaphoreType.DMA
    hbm = pl.BlockSpec(memory_space=pl.ANY)
    vmem = pl.BlockSpec(memory_space=pltpu.VMEM)
    return pl.pallas_call(
        kernel,
        out_shape=(
            jax.ShapeDtypeStruct((tok, cols), BF16),
            jax.ShapeDtypeStruct((rows, cols), F32),
            jax.ShapeDtypeStruct((rows, cols), BF16),
        ),
        in_specs=[pl.BlockSpec(memory_space=pltpu.SMEM), hbm, hbm, hbm, hbm],
        out_specs=(hbm, vmem, vmem),
        scratch_shapes=[
            pltpu.VMEM((2 * tok, depth), BF16),
            pltpu.VMEM((depth, half), BF16),
            pltpu.VMEM((padded, NZ * rows), BF16),
            pltpu.VMEM((NZ * rows, padded), BF16),
            pltpu.VMEM((padded, cols), BF16),
            pltpu.VMEM((NZ * rows, cols), BF16),
            pltpu.VMEM((4, rows, wide), BF16),
            pltpu.VMEM((3, rows, narrow), BF16),
            pltpu.VMEM((3, rows, wide), BF16),
            pltpu.VMEM((4, rows, narrow), BF16),
            pltpu.VMEM((2 * tok, half), BF16),
            pltpu.VMEM((rows, cols), F32),
            pltpu.VMEM((rows, cols), BF16),
            pltpu.VMEM((NGROUP, rows // 8, 512), BF16),
            pltpu.VMEM((NGROUP, rows // 8, 512), BF16),
            pltpu.VMEM((NGROUP, rows // 8, 512), BF16),
            dma((6,)), dma((2,)), dma((2, 2)), dma((2, 6)), dma((2, 6)), dma((2, 2)), dma((2, 3)), dma((2, 2)),
            dma((4, 4)), dma((4, 4)), dma((2,)), dma((4, 4)), dma((4, 4)), dma((3,)), dma, dma, dma, dma,
        ],
        compiler_params=pltpu.CompilerParams(
            collective_id=0, has_side_effects=True, vmem_limit_bytes=60 * 2**20
        ),
    )(inverse, inputs, weight, out_grad, master)


def on_device(inputs, weight, out_grad, master, moment_one, moment_two, partner):
    labels = jnp.arange(NGROUP, dtype=jnp.int32)
    matches = (partner[None, :] == labels[:, None]).astype(jnp.int32)
    inverse = jnp.sum(matches * labels[None, :], axis=1)
    activations, gradient, copied = exchange(inverse, inputs, weight, out_grad, master)
    new_one = 0.9 * moment_one + 0.1 * gradient
    new_two = 0.95 * moment_two + 0.05 * gradient * gradient
    new_master = master - 0.0003 * (new_one / (jnp.sqrt(new_two) + 1e-08) + 0.1 * master)
    return (activations, new_master, new_one, new_two, copied.astype(F32))


def solution(mesh):
    split = P("group", "local")
    return jax.shard_map(
        on_device,
        mesh=mesh,
        in_specs=(P("group", None), P(("group", "local"), None), split, split, split, split, P()),
        out_specs=(split,) * 5,
        check_vma=False,
    )
```

```python
import jax
import jax.numpy as jnp
from jax import lax
from jax.experimental import pallas as pl
from jax.experimental.pallas import tpu as pltpu
from jax.sharding import PartitionSpec as P

NZ = 8
NX = 4
NLOCAL = 8
NGROUP = 32
BF16 = jnp.bfloat16
F32 = jnp.float32


def group_of(yl, z, c):
    return (yl * NZ + z) * 2 + c


def local_of(x, yh):
    return x * 2 + yh


def kernel(
    partner, x_hbm, w_hbm, og_hbm, ms_hbm,
    act, grad, bk,
    xs, wt, xq, xt, og, dw, rp0, rp1, rm0, rm1, ob, ms, mb, r1, s2, b2,
    inverse, load_sem, aw_sem, yo_sem, xp_sem, xm_sem, yg_sem, sg_sem, sq_sem,
    agr_sem, ags_sem, sw_sem, rsr_sem, rss_sem, ao_sem, b1r_sem, b1s_sem, b2r_sem, b2s_sem,
):
    g, l = lax.axis_index("group"), lax.axis_index("local")
    yl, z, c = g // (2 * NZ), (g // 2) % NZ, g % 2
    x, yh = l // 2, l % 2
    tok, depth = x_hbm.shape
    cols = og_hbm.shape[1]
    half = cols // 2
    rows = ms_hbm.shape[0]
    wrows = w_hbm.shape[0]
    slice_cols = depth // NX
    piece = slice_cols // 2
    total = 4 * tok
    padded = og.shape[0]
    wide, narrow = rp0.shape[2], rp1.shape[2]
    bh, bw = r1.shape[1], r1.shape[2]
    bwidth = [bw, bw, bw, cols - 3 * bw]

    sister = (group_of(yl, z, 1 - c), l)
    y_near = (group_of(1 - yl, z, c), l)
    y_far = (group_of(1 - yl, z, c), local_of(x, 1 - yh))
    z_up, z_down = (group_of(yl, (z + 1) % NZ, c), l), (group_of(yl, (z + NZ - 1) % NZ, c), l)
    x_up, x_down = (g, local_of((x + 1) % NX, yh)), (g, local_of((x + NX - 1) % NX, yh))

    def send(src, dst, ssem, rsem, device):
        copy = pltpu.make_async_remote_copy(
            src_ref=src, dst_ref=dst, send_sem=ssem, recv_sem=rsem,
            device_id=device, device_id_type=pl.DeviceIdType.MESH,
        )
        copy.start()
        return copy

    def wait_bytes(like, sem):
        pltpu.make_async_copy(like, like, sem).wait()

    def aligned(at, size):
        return pl.ds(pl.multiple_of(at, size), size)

    load_x = pltpu.make_async_copy(x_hbm, xs.at[pl.ds(0, tok)], load_sem.at[0])
    load_og = pltpu.make_async_copy(og_hbm, og.at[pl.ds(0, tok)], load_sem.at[1])
    load_ms = pltpu.make_async_copy(ms_hbm, ms, load_sem.at[2])
    load_ms.start()
    load_x.start()
    load_og.start()
    own_w = pltpu.make_async_copy(
        w_hbm.at[:, aligned(l * cols + yl * half, 128 * 7)],
        wt.at[aligned((g * NLOCAL + l) * wrows, wrows)],
        load_sem.at[3],
    )
    own_w.start()

    def own_block(zb, core):
        return aligned((yl * 2 * NZ + zb * 2 + core) * 128, 128)

    @pl.loop(0, NZ)
    def _(zb):
        pltpu.make_async_copy(
            x_hbm.at[:, own_block(zb, c)], xq.at[pl.ds(0, tok), aligned(zb * 128, 128)], load_sem.at[4]
        ).start()

    barrier = pltpu.get_barrier_semaphore()

    @pl.loop(1, NGROUP)
    def _(o):
        pl.semaphore_signal(
            barrier, inc=1, device_id=((g + o) % NGROUP, l), device_id_type=pl.DeviceIdType.MESH
        )

    @pl.loop(2, 2 * NLOCAL)
    def _(o):
        pl.semaphore_signal(
            barrier, inc=1,
            device_id=(group_of((yl + o) % 2, z, c), (l + o // 2) % NLOCAL),
            device_id_type=pl.DeviceIdType.MESH,
        )

    load_ms.wait()
    mb[...] = ms[...].astype(BF16)
    og[pl.ds(total, padded - total), :] = jnp.zeros((padded - total, cols), BF16)
    xq[pl.ds(total, padded - total), :] = jnp.zeros((padded - total, xq.shape[1]), BF16)
    pl.semaphore_wait(barrier, NGROUP - 1 + 2 * NLOCAL - 2)

    my_rows = aligned((g * NLOCAL + l) * wrows, wrows)

    @pl.loop(1, 2 * NLOCAL)
    def _(o):
        to_l, to_y = (l + o // 2) % NLOCAL, (yl + o) % 2
        send(
            w_hbm.at[:, aligned(to_l * cols + to_y * half, 128 * 7)], wt.at[my_rows],
            aw_sem.at[0], aw_sem.at[1], (group_of(to_y, z, c), to_l),
        )

    def x_columns(side, at, sub, n):
        return aligned(side * (depth // 2) + ((at + NX) % NX) * piece + sub * (piece // 2), n * (piece // 2))

    def far_send(p, side):
        ref = x_hbm.at[:, x_columns(side, x, 0, 2)]
        return send(ref, xs.at[pl.ds(tok, tok), x_columns(side, x, 0, 2)], yo_sem.at[0, p], yo_sem.at[1, p], y_far)

    og_cut = [(0, wide), (wide, narrow)]

    def near_send(p):
        at, n = og_cut[p]
        return send(
            og_hbm.at[:, pl.ds(at, n)], og.at[pl.ds(2 * tok, tok), pl.ds(at, n)],
            yg_sem.at[0, p], yg_sem.at[1, p], y_near,
        )

    far = [far_send(0, 1 - yl)]
    near = [near_send(0)]

    last = g % 4 == 3

    @pl.loop(0, NGROUP // 4)
    def _(q):
        for r in range(4):
            i, n = 4 * q + r, bwidth[r]
            src = mb.at[aligned(q * bh, bh), pl.ds(bw * r, n)]

            @pl.when(g != i)
            def _():
                send(src, r1.at[g, :, pl.ds(0, n)], b1s_sem.at[r // 3], b1r_sem, (i, l))

            @pl.when(g == i)
            def _():
                r1[i, :, pl.ds(0, n)] = src[...]

    far.append(far_send(1, yl))
    near.append(near_send(1))
    og_own = send(og_hbm, og.at[pl.ds(tok, tok)], sg_sem.at[0, 0], sg_sem.at[1, 0], sister)

    @pl.loop(0, NZ)
    def _(zb):
        send(
            x_hbm.at[:, own_block(zb, 1 - c)], xq.at[pl.ds(tok, tok), aligned(zb * 128, 128)],
            sq_sem.at[0, 0], sq_sem.at[1, 0], sister,
        )

    @pl.loop(0, NGROUP)
    def _(j):
        found = jnp.int32(0)
        for i in range(NGROUP):
            found = jnp.where(partner[i] == j, i, found)
        inverse[j] = found

    def by_width(do):
        pl.when(last)(lambda: do(bwidth[3]))
        pl.when(jnp.logical_not(last))(lambda: do(bw))

    def wait_own(ref, sem):
        by_width(lambda n: wait_bytes(ref.at[pl.ds(0, NGROUP - 1), :, pl.ds(0, n)], sem))

    def wait_all(ref, sem):
        full, rest = NGROUP // 4 * 3, NGROUP // 4

        def do(n):
            wait_bytes(ref.at[pl.ds(0, full - (n == bw))], sem.at[0])
            wait_bytes(ref.at[pl.ds(0, rest - (n != bw)), :, pl.ds(0, bwidth[3])], sem.at[1])

        by_width(do)

    def w_block(h, at):
        return wt.at[aligned((h * 2 * NZ + at * 2 + c) * 128, 128)]

    chains = [(0, 1, 0, 4), (1, -1, 1, 4), (2, 1, 1, 3), (3, -1, 0, 3)]
    later = []

    def w_send(k, way, h, s):
        block = w_block(h, (z - way * s + NZ) % NZ)
        copy = send(block, block, ags_sem.at[k, s], agr_sem.at[k, s], z_up if way > 0 else z_down)
        later.append(copy)

    def w_sister(h, at):
        block = w_block(h, at)
        send(block, block, sw_sem.at[0], sw_sem.at[1], sister)

    def w_arrive(s, some):
        for k, way, h, n in chains:
            if k in some and s < n:
                at = (z - way * (s + 1) + NZ) % NZ
                wait_bytes(w_block(h, at), agr_sem.at[k, s])
                if s + 1 < n:
                    w_send(k, way, h, s + 1)
                w_sister(h, at)

    own_w.wait()
    wait_bytes(wt.at[pl.ds(0, 15 * wrows)], aw_sem.at[1])
    for k, way, h, n in chains:
        w_send(k, way, h, 0)
    for h in range(2):
        w_sister(h, z)

    def x_piece(at, p, sub):
        return xs.at[pl.ds(tok, tok), x_columns(yl if p == 0 else 1 - yl, at, sub, 1)]

    def x_send(way, at, p, sub, n):
        ref, sem = x_piece(at, p, sub), xp_sem if way > 0 else xm_sem
        later.append(send(ref, ref, sem.at[0, 3 * p + n], sem.at[1, 3 * p + n], x_up if way > 0 else x_down))

    def x_own(p):
        far[p].wait_recv()
        x_send(1, x, p, 0, 0)
        x_send(-1, x, p, 1, 0)
        x_send(1, x, p, 1, 1)
        x_send(-1, x, p, 0, 1)

    def x_forward(p):
        wait_bytes(x_piece(x, p, 0), xp_sem.at[1, 3 * p])
        x_send(1, x - 1, p, 0, 2)
        wait_bytes(x_piece(x, p, 1), xm_sem.at[1, 3 * p])
        x_send(-1, x + 1, p, 1, 2)

    def x_complete(p):
        for sem in (xp_sem, xm_sem):
            for n in (1, 2):
                wait_bytes(x_piece(x, p, 0), sem.at[1, 3 * p + n])

    def og_forward(p):
        near[p].wait_recv()
        at, n = og_cut[p]
        later.append(
            send(
                og.at[pl.ds(2 * tok, tok), pl.ds(at, n)], og.at[pl.ds(3 * tok, tok), pl.ds(at, n)],
                sg_sem.at[0, 1 + p], sg_sem.at[1, 1 + p], sister,
            )
        )

    def og_arrive(p):
        at, n = og_cut[p]
        wait_bytes(og.at[pl.ds(0, tok), pl.ds(at, n)], sg_sem.at[1, 1 + p])

    early = 2 * tok // 128 * 128

    def turn(at, n):
        @pl.loop(0, NZ)
        def _(zb):
            xt[aligned(zb * 128, 128), pl.ds(at, n)] = xq[pl.ds(at, n), aligned(zb * 128, 128)].T

    def dw_chunk(j):
        at = aligned(j * 256, 256)
        dw[:, at] = jnp.dot(xt[...], og[:, at], preferred_element_type=F32).astype(BF16)

    def dw_block(d, h):
        return dw.at[aligned(((d + 2 * NZ) % NZ) * rows, rows), pl.ds(0, wide) if h == 0 else pl.ds(wide, narrow)]

    rs_bufs = [rp0, rm1, rp1, rm0]

    def r_send(k, way, h, n, s):
        src = dw_block(z + way * n, h) if s == 0 else rs_bufs[k].at[s - 1]
        later.append(
            send(src, rs_bufs[k].at[s], rss_sem.at[k, s], rsr_sem.at[k, s], z_up if way > 0 else z_down)
        )

    def r_arrive(s, some):
        for k, way, h, n in chains:
            if k in some and s < n:
                buf = rs_bufs[k]
                wait_bytes(buf.at[s], rsr_sem.at[k, s])
                if s + 1 < n:
                    mine = dw_block(z + way * (n - s - 1), h)
                    buf[s] = (buf[s].astype(F32) + mine[...].astype(F32)).astype(BF16)
                    r_send(k, way, h, n, s + 1)

    def act_chunk(at, n):
        ob[:, pl.ds(at, n)] = jnp.dot(
            xs[...], wt[:, pl.ds(at, n)], preferred_element_type=F32
        ).astype(BF16)

    wait_bytes(xq.at[pl.ds(0, tok)], sq_sem.at[1, 0])
    wait_bytes(xq.at[pl.ds(0, tok)], load_sem.at[4])
    turn(0, early)
    x_own(0)
    w_arrive(0, (0, 1))
    x_forward(0)
    w_arrive(0, (2, 3))
    x_own(1)
    w_arrive(1, (0, 1))
    og_forward(0)
    x_complete(0)

    @pl.loop(0, NZ)
    def _(zb):
        send(
            xs.at[pl.ds(tok, tok), own_block(zb, 1 - c)],
            xq.at[pl.ds(3 * tok, tok), aligned(zb * 128, 128)],
            sq_sem.at[0, 1], sq_sem.at[1, 1], sister,
        )
        pltpu.make_async_copy(
            xs.at[pl.ds(tok, tok), own_block(zb, c)],
            xq.at[pl.ds(2 * tok, tok), aligned(zb * 128, 128)],
            load_sem.at[5],
        ).start()

    w_arrive(1, (2, 3))

    load_og.wait()
    og_own.wait_recv()
    wait_bytes(xq.at[pl.ds(0, tok)], sq_sem.at[1, 1])
    wait_bytes(xq.at[pl.ds(0, tok)], load_sem.at[5])
    turn(early, padded - early)
    og_arrive(0)
    pl.loop(0, wide // 256)(dw_chunk)
    r_send(0, 1, 0, 4, 0)
    r_send(3, -1, 0, 3, 0)
    w_arrive(2, (0, 1))
    x_forward(1)
    og_forward(1)
    w_arrive(2, (2, 3))
    og_arrive(1)
    pl.loop(wide // 256, cols // 256)(dw_chunk)
    r_send(1, -1, 1, 4, 0)
    r_send(2, 1, 1, 3, 0)
    w_arrive(3, (0, 1))

    wait_own(r1, b1r_sem)

    @pl.loop(0, NGROUP)
    def _(j):
        s2[j] = r1[inverse[j]]

    def second_exchange(n):
        @pl.loop(0, NGROUP)
        def _(j):
            @pl.when(g != j)
            def _():
                send(
                    s2.at[j, :, pl.ds(0, n)], b2.at[g, :, pl.ds(0, n)],
                    b2s_sem, b2r_sem.at[0 if n == bw else 1], (j, l),
                )

        b2[g, :, pl.ds(0, n)] = s2[g, :, pl.ds(0, n)]

    by_width(second_exchange)

    load_x.wait()
    x_complete(1)
    wait_bytes(wt.at[pl.ds(0, depth // 2)], sw_sem.at[1])
    act_chunk(0, 256)
    r_arrive(0, (0, 3))
    act_chunk(256, 256)
    r_arrive(0, (1, 2))
    act_chunk(512, 256)
    act_chunk(768, 128)
    their = send(
        ob.at[pl.ds(tok, tok)], act.at[:, aligned(yl * half, half)], ao_sem.at[0], ao_sem.at[1], y_near
    )
    own_act = pltpu.make_async_copy(
        ob.at[pl.ds(0, tok)], act.at[:, aligned(yl * half, half)], ao_sem.at[2]
    )
    own_act.start()
    r_arrive(1, (0, 3))
    r_arrive(1, (1, 2))
    r_arrive(2, (0, 3))
    r_arrive(2, (1, 2))

    wait_all(b2, b2r_sem)

    @pl.loop(0, NGROUP // 4)
    def _(q):
        for r in range(4):
            bk[aligned(q * bh, bh), pl.ds(bw * r, bwidth[r])] = b2[4 * q + r, :, pl.ds(0, bwidth[r])]

    r_arrive(3, (0, 1))
    mine = dw[aligned(z * rows, rows), :].astype(F32)
    grad[:, pl.ds(0, wide)] = mine[:, :wide] + rp0[3].astype(F32) + rm0[2].astype(F32)
    grad[:, pl.ds(wide, narrow)] = mine[:, wide:] + rp1[2].astype(F32) + rm1[3].astype(F32)

    wait_bytes(wt.at[pl.ds(0, 15 * wrows)], aw_sem.at[0])
    for copy in far + near + later + [og_own]:
        copy.wait_send()
    for n in range(2):
        wait_bytes(xq.at[pl.ds(0, tok)], sq_sem.at[0, n])
    wait_bytes(wt.at[pl.ds(0, depth // 2)], sw_sem.at[0])
    wait_all(r1, b1s_sem)
    wait_own(b2, b2s_sem)
    their.wait()
    own_act.wait()


def exchange(partner, inputs, weight, out_grad, master):
    tok, depth = inputs.shape
    cols = out_grad.shape[1]
    rows = master.shape[0]
    padded = -(-4 * tok // 256) * 256
    half = cols // 2
    wide = (cols // 256 + 1) // 2 * 256
    narrow = cols - wide
    dma = pltpu.SemaphoreType.DMA
    hbm = pl.BlockSpec(memory_space=pl.ANY)
    vmem = pl.BlockSpec(memory_space=pltpu.VMEM)
    return pl.pallas_call(
        kernel,
        out_shape=(
            jax.ShapeDtypeStruct((tok, cols), BF16),
            jax.ShapeDtypeStruct((rows, cols), F32),
            jax.ShapeDtypeStruct((rows, cols), BF16),
        ),
        in_specs=[pl.BlockSpec(memory_space=pltpu.SMEM), hbm, hbm, hbm, hbm],
        out_specs=(hbm, vmem, vmem),
        scratch_shapes=[
            pltpu.VMEM((2 * tok, depth), BF16),
            pltpu.VMEM((depth, half), BF16),
            pltpu.VMEM((padded, NZ * rows), BF16),
            pltpu.VMEM((NZ * rows, padded), BF16),
            pltpu.VMEM((padded, cols), BF16),
            pltpu.VMEM((NZ * rows, cols), BF16),
            pltpu.VMEM((4, rows, wide), BF16),
            pltpu.VMEM((3, rows, narrow), BF16),
            pltpu.VMEM((3, rows, wide), BF16),
            pltpu.VMEM((4, rows, narrow), BF16),
            pltpu.VMEM((2 * tok, half), BF16),
            pltpu.VMEM((rows, cols), F32),
            pltpu.VMEM((rows, cols), BF16),
            pltpu.VMEM((NGROUP, rows // 8, 512), BF16),
            pltpu.VMEM((NGROUP, rows // 8, 512), BF16),
            pltpu.VMEM((NGROUP, rows // 8, 512), BF16),
            pltpu.SMEM((NGROUP,), jnp.int32),
            dma((6,)), dma((2,)), dma((2, 2)), dma((2, 6)), dma((2, 6)), dma((2, 2)), dma((2, 3)), dma((2, 2)),
            dma((4, 4)), dma((4, 4)), dma((2,)), dma((4, 4)), dma((4, 4)), dma((3,)), dma, dma((2,)), dma((2,)), dma,
        ],
        compiler_params=pltpu.CompilerParams(
            collective_id=0, has_side_effects=True, vmem_limit_bytes=60 * 2**20
        ),
    )(partner, inputs, weight, out_grad, master)


def on_device(inputs, weight, out_grad, master, moment_one, moment_two, partner):
    activations, gradient, copied = exchange(partner, inputs, weight, out_grad, master)
    new_one = 0.9 * moment_one + 0.1 * gradient
    new_two = 0.95 * moment_two + 0.05 * gradient * gradient
    new_master = master - 0.0003 * (new_one / (jnp.sqrt(new_two) + 1e-08) + 0.1 * master)
    return (activations, new_master, new_one, new_two, copied.astype(F32))


def solution(mesh):
    split = P("group", "local")
    return jax.shard_map(
        on_device,
        mesh=mesh,
        in_specs=(P("group", None), P(("group", "local"), None), split, split, split, split, P()),
        out_specs=(split,) * 5,
        check_vma=False,
    )
```

```python
import jax
import jax.numpy as jnp
from jax import lax
from jax.experimental import pallas as pl
from jax.experimental.pallas import tpu as pltpu
from jax.sharding import PartitionSpec as P

NZ = 8
NX = 4
NLOCAL = 8
NGROUP = 32
BF16 = jnp.bfloat16
F32 = jnp.float32


def group_of(yl, z, c):
    return (yl * NZ + z) * 2 + c


def local_of(x, yh):
    return x * 2 + yh


def kernel(
    partner, x_hbm, w_hbm, og_hbm, ms_hbm,
    act, grad, bk,
    xs, wt, xq, xt, og, dw, rp0, rp1, rm0, rm1, ob, ms, mb, r1, s2, b2,
    inverse, load_sem, aw_sem, yo_sem, xp_sem, xm_sem, yg_sem, sg_sem, sq_sem,
    agr_sem, ags_sem, sw_sem, rsr_sem, rss_sem, ao_sem, b1r_sem, b1s_sem, b2r_sem, b2s_sem,
):
    g, l = lax.axis_index("group"), lax.axis_index("local")
    yl, z, c = g // (2 * NZ), (g // 2) % NZ, g % 2
    x, yh = l // 2, l % 2
    tok, depth = x_hbm.shape
    cols = og_hbm.shape[1]
    half = cols // 2
    rows = ms_hbm.shape[0]
    wrows = w_hbm.shape[0]
    slice_cols = depth // NX
    piece = slice_cols // 2
    total = 4 * tok
    padded = og.shape[0]
    wide = (cols // 256 + 1) // 2 * 256
    narrow = cols - wide
    bh, bw = r1.shape[1], r1.shape[2]
    bwidth = [bw, bw, bw, cols - 3 * bw]

    sister = (group_of(yl, z, 1 - c), l)
    y_near = (group_of(1 - yl, z, c), l)
    y_far = (group_of(1 - yl, z, c), local_of(x, 1 - yh))
    z_up, z_down = (group_of(yl, (z + 1) % NZ, c), l), (group_of(yl, (z + NZ - 1) % NZ, c), l)
    x_up, x_down = (g, local_of((x + 1) % NX, yh)), (g, local_of((x + NX - 1) % NX, yh))

    def send(src, dst, ssem, rsem, device):
        copy = pltpu.make_async_remote_copy(
            src_ref=src, dst_ref=dst, send_sem=ssem, recv_sem=rsem,
            device_id=device, device_id_type=pl.DeviceIdType.MESH,
        )
        copy.start()
        return copy

    def wait_bytes(like, sem):
        pltpu.make_async_copy(like, like, sem).wait()

    def aligned(at, size):
        return pl.ds(pl.multiple_of(at, size), size)

    barrier = pltpu.get_barrier_semaphore()

    @pl.loop(1, NGROUP)
    def _(o):
        pl.semaphore_signal(
            barrier, inc=1, device_id=((g + o) % NGROUP, l), device_id_type=pl.DeviceIdType.MESH
        )

    @pl.loop(2, 2 * NLOCAL)
    def _(o):
        pl.semaphore_signal(
            barrier, inc=1,
            device_id=(group_of((yl + o) % 2, z, c), (l + o // 2) % NLOCAL),
            device_id_type=pl.DeviceIdType.MESH,
        )

    load_x = pltpu.make_async_copy(x_hbm, xs.at[pl.ds(0, tok)], load_sem.at[0])
    load_og = pltpu.make_async_copy(og_hbm, og.at[pl.ds(0, tok)], load_sem.at[1])
    load_ms = pltpu.make_async_copy(ms_hbm, ms, load_sem.at[2])
    load_ms.start()
    load_x.start()
    load_og.start()
    own_w = pltpu.make_async_copy(
        w_hbm.at[:, aligned(l * cols + yl * half, 128 * 7)],
        wt.at[aligned((g * NLOCAL + l) * wrows, wrows)],
        load_sem.at[3],
    )
    own_w.start()

    def own_block(zb, core):
        return aligned((yl * 2 * NZ + zb * 2 + core) * 128, 128)

    @pl.loop(0, NZ)
    def _(zb):
        pltpu.make_async_copy(
            x_hbm.at[:, own_block(zb, c)], xq.at[pl.ds(0, tok), aligned(zb * 128, 128)], load_sem.at[4]
        ).start()

    og[pl.ds(total, padded - total), :] = jnp.zeros((padded - total, cols), BF16)
    xq[pl.ds(total, padded - total), :] = jnp.zeros((padded - total, xq.shape[1]), BF16)
    pl.semaphore_wait(barrier, NGROUP - 1 + 2 * NLOCAL - 2)

    my_rows = aligned((g * NLOCAL + l) * wrows, wrows)

    @pl.loop(1, 2 * NLOCAL)
    def _(o):
        to_l, to_y = (l + o // 2) % NLOCAL, (yl + o) % 2
        send(
            w_hbm.at[:, aligned(to_l * cols + to_y * half, 128 * 7)], wt.at[my_rows],
            aw_sem.at[0], aw_sem.at[1], (group_of(to_y, z, c), to_l),
        )

    def x_columns(side, at, sub, n):
        return aligned(side * (depth // 2) + ((at + NX) % NX) * piece + sub * (piece // 2), n * (piece // 2))

    def far_send(p, side):
        ref = x_hbm.at[:, x_columns(side, x, 0, 2)]
        return send(ref, xs.at[pl.ds(tok, tok), x_columns(side, x, 0, 2)], yo_sem.at[0, p], yo_sem.at[1, p], y_far)

    og_cut = [(0, wide), (wide, narrow)]

    def near_send(p):
        at, n = og_cut[p]
        return send(
            og_hbm.at[:, pl.ds(at, n)], og.at[pl.ds(2 * tok, tok), pl.ds(at, n)],
            yg_sem.at[0, p], yg_sem.at[1, p], y_near,
        )

    far = [far_send(0, 1 - yl)]
    near = [near_send(0)]

    last = g % 4 == 3
    load_ms.wait()
    mb[...] = ms[...].astype(BF16)

    @pl.loop(0, NGROUP // 4)
    def _(q):
        for r in range(4):
            i, n = 4 * q + r, bwidth[r]
            src = mb.at[aligned(q * bh, bh), pl.ds(bw * r, n)]

            @pl.when(g != i)
            def _():
                send(src, r1.at[g, :, pl.ds(0, n)], b1s_sem.at[r // 3], b1r_sem, (i, l))

            @pl.when(g == i)
            def _():
                r1[i, :, pl.ds(0, n)] = src[...]

    far.append(far_send(1, yl))
    near.append(near_send(1))
    og_own = send(og_hbm, og.at[pl.ds(tok, tok)], sg_sem.at[0, 0], sg_sem.at[1, 0], sister)

    @pl.loop(0, NZ)
    def _(zb):
        send(
            x_hbm.at[:, own_block(zb, 1 - c)], xq.at[pl.ds(tok, tok), aligned(zb * 128, 128)],
            sq_sem.at[0, 0], sq_sem.at[1, 0], sister,
        )

    @pl.loop(0, NGROUP)
    def _(j):
        found = jnp.int32(0)
        for i in range(NGROUP):
            found = jnp.where(partner[i] == j, i, found)
        inverse[j] = found

    def by_width(do):
        pl.when(last)(lambda: do(bwidth[3]))
        pl.when(jnp.logical_not(last))(lambda: do(bw))

    def wait_own(ref, sem):
        by_width(lambda n: wait_bytes(ref.at[pl.ds(0, NGROUP - 1), :, pl.ds(0, n)], sem))

    def wait_all(ref, sem):
        full, rest = NGROUP // 4 * 3, NGROUP // 4

        def do(n):
            wait_bytes(ref.at[pl.ds(0, full - (n == bw))], sem.at[0])
            wait_bytes(ref.at[pl.ds(0, rest - (n != bw)), :, pl.ds(0, bwidth[3])], sem.at[1])

        by_width(do)

    def w_block(h, at):
        return wt.at[aligned((h * 2 * NZ + at * 2 + c) * 128, 128)]

    chains = [(0, 1, 0, 4), (1, -1, 1, 4), (2, 1, 1, 3), (3, -1, 0, 3)]
    later = []

    def w_send(k, way, h, s):
        block = w_block(h, (z - way * s + NZ) % NZ)
        copy = send(block, block, ags_sem.at[k, s], agr_sem.at[k, s], z_up if way > 0 else z_down)
        later.append(copy)

    def w_sister(h, at):
        block = w_block(h, at)
        send(block, block, sw_sem.at[0], sw_sem.at[1], sister)

    def w_arrive(s, some):
        for k, way, h, n in chains:
            if k in some and s < n:
                at = (z - way * (s + 1) + NZ) % NZ
                wait_bytes(w_block(h, at), agr_sem.at[k, s])
                if s + 1 < n:
                    w_send(k, way, h, s + 1)
                w_sister(h, at)

    own_w.wait()
    wait_bytes(wt.at[pl.ds(0, 15 * wrows)], aw_sem.at[1])
    for k, way, h, n in chains:
        w_send(k, way, h, 0)
    for h in range(2):
        w_sister(h, z)

    def x_piece(at, p, sub):
        return xs.at[pl.ds(tok, tok), x_columns(yl if p == 0 else 1 - yl, at, sub, 1)]

    def x_send(way, at, p, sub, n):
        ref, sem = x_piece(at, p, sub), xp_sem if way > 0 else xm_sem
        later.append(send(ref, ref, sem.at[0, 3 * p + n], sem.at[1, 3 * p + n], x_up if way > 0 else x_down))

    def x_own(p):
        far[p].wait_recv()
        x_send(1, x, p, 0, 0)
        x_send(-1, x, p, 1, 0)
        x_send(1, x, p, 1, 1)
        x_send(-1, x, p, 0, 1)

    def x_forward(p):
        wait_bytes(x_piece(x, p, 0), xp_sem.at[1, 3 * p])
        x_send(1, x - 1, p, 0, 2)
        wait_bytes(x_piece(x, p, 1), xm_sem.at[1, 3 * p])
        x_send(-1, x + 1, p, 1, 2)

    def x_complete(p):
        for sem in (xp_sem, xm_sem):
            for n in (1, 2):
                wait_bytes(x_piece(x, p, 0), sem.at[1, 3 * p + n])

    def og_forward(p):
        near[p].wait_recv()
        at, n = og_cut[p]
        later.append(
            send(
                og.at[pl.ds(2 * tok, tok), pl.ds(at, n)], og.at[pl.ds(3 * tok, tok), pl.ds(at, n)],
                sg_sem.at[0, 1 + p], sg_sem.at[1, 1 + p], sister,
            )
        )

    def og_arrive(p):
        at, n = og_cut[p]
        wait_bytes(og.at[pl.ds(0, tok), pl.ds(at, n)], sg_sem.at[1, 1 + p])

    early = 2 * tok // 128 * 128

    def turn(at, n):
        @pl.loop(0, NZ)
        def _(zb):
            xt[aligned(zb * 128, 128), pl.ds(at, n)] = xq[pl.ds(at, n), aligned(zb * 128, 128)].T

    def dw_chunk(j):
        at = aligned(j * 256, 256)
        dw[:, at] = jnp.dot(xt[...], og[:, at], preferred_element_type=F32).astype(BF16)

    def dw_block(d, h):
        return dw.at[aligned(((d + 2 * NZ) % NZ) * rows, rows), pl.ds(h * half, half)]

    rs_bufs = [rp0, rm1, rp1, rm0]

    def r_send(k, way, h, n, s):
        src = dw_block(z + way * n, h) if s == 0 else rs_bufs[k].at[s - 1]
        later.append(
            send(src, rs_bufs[k].at[s], rss_sem.at[k, s], rsr_sem.at[k, s], z_up if way > 0 else z_down)
        )

    def r_arrive(s, some):
        for k, way, h, n in chains:
            if k in some and s < n:
                buf = rs_bufs[k]
                wait_bytes(buf.at[s], rsr_sem.at[k, s])
                if s + 1 < n:
                    mine = dw_block(z + way * (n - s - 1), h)
                    buf[s] = (buf[s].astype(F32) + mine[...].astype(F32)).astype(BF16)
                    r_send(k, way, h, n, s + 1)

    def act_chunk(at, n):
        ob[:, pl.ds(at, n)] = jnp.dot(
            xs[...], wt[:, pl.ds(at, n)], preferred_element_type=F32
        ).astype(BF16)

    wait_bytes(xq.at[pl.ds(0, tok)], sq_sem.at[1, 0])
    wait_bytes(xq.at[pl.ds(0, tok)], load_sem.at[4])
    turn(0, early)
    x_own(0)
    w_arrive(0, (0, 1))
    x_forward(0)
    w_arrive(0, (2, 3))
    x_own(1)
    w_arrive(1, (0, 1))
    og_forward(0)
    x_complete(0)

    @pl.loop(0, NZ)
    def _(zb):
        send(
            xs.at[pl.ds(tok, tok), own_block(zb, 1 - c)],
            xq.at[pl.ds(3 * tok, tok), aligned(zb * 128, 128)],
            sq_sem.at[0, 1], sq_sem.at[1, 1], sister,
        )
        pltpu.make_async_copy(
            xs.at[pl.ds(tok, tok), own_block(zb, c)],
            xq.at[pl.ds(2 * tok, tok), aligned(zb * 128, 128)],
            load_sem.at[5],
        ).start()

    w_arrive(1, (2, 3))

    load_og.wait()
    og_own.wait_recv()
    wait_bytes(xq.at[pl.ds(0, tok)], sq_sem.at[1, 1])
    wait_bytes(xq.at[pl.ds(0, tok)], load_sem.at[5])
    turn(early, padded - early)
    w_arrive(2, (0, 1))
    og_arrive(0)
    pl.loop(0, wide // 256)(dw_chunk)
    r_send(0, 1, 0, 4, 0)
    r_send(3, -1, 0, 3, 0)
    x_forward(1)
    og_forward(1)
    w_arrive(2, (2, 3))
    og_arrive(1)
    pl.loop(wide // 256, cols // 256)(dw_chunk)
    r_send(1, -1, 1, 4, 0)
    r_send(2, 1, 1, 3, 0)
    w_arrive(3, (0, 1))

    wait_own(r1, b1r_sem)

    @pl.loop(0, NGROUP)
    def _(j):
        s2[j] = r1[inverse[j]]

    def second_exchange(n):
        @pl.loop(0, NGROUP)
        def _(j):
            @pl.when(g != j)
            def _():
                send(
                    s2.at[j, :, pl.ds(0, n)], b2.at[g, :, pl.ds(0, n)],
                    b2s_sem, b2r_sem.at[0 if n == bw else 1], (j, l),
                )

        b2[g, :, pl.ds(0, n)] = s2[g, :, pl.ds(0, n)]

    by_width(second_exchange)

    load_x.wait()
    x_complete(1)
    wait_bytes(wt.at[pl.ds(0, depth // 2)], sw_sem.at[1])
    act_chunk(0, 256)
    r_arrive(0, (0, 3))
    act_chunk(256, 256)
    r_arrive(0, (1, 2))
    act_chunk(512, 256)
    act_chunk(768, 128)
    their = send(
        ob.at[pl.ds(tok, tok)], act.at[:, aligned(yl * half, half)], ao_sem.at[0], ao_sem.at[1], y_near
    )
    own_act = pltpu.make_async_copy(
        ob.at[pl.ds(0, tok)], act.at[:, aligned(yl * half, half)], ao_sem.at[2]
    )
    own_act.start()
    r_arrive(1, (0, 3))
    r_arrive(1, (1, 2))
    r_arrive(2, (0, 3))
    r_arrive(2, (1, 2))

    wait_all(b2, b2r_sem)

    @pl.loop(0, NGROUP // 4)
    def _(q):
        for r in range(4):
            bk[aligned(q * bh, bh), pl.ds(bw * r, bwidth[r])] = b2[4 * q + r, :, pl.ds(0, bwidth[r])]

    r_arrive(3, (0, 1))
    mine = dw[aligned(z * rows, rows), :].astype(F32)
    grad[:, pl.ds(0, half)] = mine[:, :half] + rp0[3].astype(F32) + rm0[2].astype(F32)
    grad[:, pl.ds(half, half)] = mine[:, half:] + rp1[2].astype(F32) + rm1[3].astype(F32)

    wait_bytes(wt.at[pl.ds(0, 15 * wrows)], aw_sem.at[0])
    for copy in far + near + later + [og_own]:
        copy.wait_send()
    for n in range(2):
        wait_bytes(xq.at[pl.ds(0, tok)], sq_sem.at[0, n])
    wait_bytes(wt.at[pl.ds(0, depth // 2)], sw_sem.at[0])
    wait_all(r1, b1s_sem)
    wait_own(b2, b2s_sem)
    their.wait()
    own_act.wait()


def exchange(partner, inputs, weight, out_grad, master):
    tok, depth = inputs.shape
    cols = out_grad.shape[1]
    rows = master.shape[0]
    padded = -(-4 * tok // 256) * 256
    half = cols // 2
    dma = pltpu.SemaphoreType.DMA
    hbm = pl.BlockSpec(memory_space=pl.ANY)
    vmem = pl.BlockSpec(memory_space=pltpu.VMEM)
    return pl.pallas_call(
        kernel,
        out_shape=(
            jax.ShapeDtypeStruct((tok, cols), BF16),
            jax.ShapeDtypeStruct((rows, cols), F32),
            jax.ShapeDtypeStruct((rows, cols), BF16),
        ),
        in_specs=[pl.BlockSpec(memory_space=pltpu.SMEM), hbm, hbm, hbm, hbm],
        out_specs=(hbm, vmem, vmem),
        scratch_shapes=[
            pltpu.VMEM((2 * tok, depth), BF16),
            pltpu.VMEM((depth, half), BF16),
            pltpu.VMEM((padded, NZ * rows), BF16),
            pltpu.VMEM((NZ * rows, padded), BF16),
            pltpu.VMEM((padded, cols), BF16),
            pltpu.VMEM((NZ * rows, cols), BF16),
            pltpu.VMEM((4, rows, half), BF16),
            pltpu.VMEM((3, rows, half), BF16),
            pltpu.VMEM((3, rows, half), BF16),
            pltpu.VMEM((4, rows, half), BF16),
            pltpu.VMEM((2 * tok, half), BF16),
            pltpu.VMEM((rows, cols), F32),
            pltpu.VMEM((rows, cols), BF16),
            pltpu.VMEM((NGROUP, rows // 8, 512), BF16),
            pltpu.VMEM((NGROUP, rows // 8, 512), BF16),
            pltpu.VMEM((NGROUP, rows // 8, 512), BF16),
            pltpu.SMEM((NGROUP,), jnp.int32),
            dma((6,)), dma((2,)), dma((2, 2)), dma((2, 6)), dma((2, 6)), dma((2, 2)), dma((2, 3)), dma((2, 2)),
            dma((4, 4)), dma((4, 4)), dma((2,)), dma((4, 4)), dma((4, 4)), dma((3,)), dma, dma((2,)), dma((2,)), dma,
        ],
        compiler_params=pltpu.CompilerParams(
            collective_id=0, has_side_effects=True, vmem_limit_bytes=60 * 2**20
        ),
    )(partner, inputs, weight, out_grad, master)


def on_device(inputs, weight, out_grad, master, moment_one, moment_two, partner):
    activations, gradient, copied = exchange(partner, inputs, weight, out_grad, master)
    new_one = 0.9 * moment_one + 0.1 * gradient
    new_two = 0.95 * moment_two + 0.05 * gradient * gradient
    new_master = master - 0.0003 * (new_one / (jnp.sqrt(new_two) + 1e-08) + 0.1 * master)
    return (activations, new_master, new_one, new_two, copied.astype(F32))


def solution(mesh):
    split = P("group", "local")
    return jax.shard_map(
        on_device,
        mesh=mesh,
        in_specs=(P("group", None), P(("group", "local"), None), split, split, split, split, P()),
        out_specs=(split,) * 5,
        check_vma=False,
    )
```

```python
import jax
import jax.numpy as jnp
from jax import lax
from jax.experimental import pallas as pl
from jax.experimental.pallas import tpu as pltpu
from jax.sharding import PartitionSpec as P

NZ = 8
NX = 4
NLOCAL = 8
NGROUP = 32
BF16 = jnp.bfloat16
F32 = jnp.float32


def group_of(yl, z, c):
    return (yl * NZ + z) * 2 + c


def local_of(x, yh):
    return x * 2 + yh


def kernel(
    partner, x_hbm, w_hbm, og_hbm, ms_hbm, m1_hbm, m2_hbm,
    act, new_ms, new_1, new_2, bk,
    xs, wt, xq, xt, og, dw, rp0, rp1, rm0, rm1, ob, ms, m1, m2, mb, r1, s2, b2,
    inverse, load_sem, aw_sem, yo_sem, xp_sem, xm_sem, yg_sem, sg_sem, sq_sem,
    agr_sem, ags_sem, sw_sem, rsr_sem, rss_sem, ao_sem, b1r_sem, b1s_sem, b2r_sem, b2s_sem,
):
    g, l = lax.axis_index("group"), lax.axis_index("local")
    yl, z, c = g // (2 * NZ), (g // 2) % NZ, g % 2
    x, yh = l // 2, l % 2
    tok, depth = x_hbm.shape
    cols = og_hbm.shape[1]
    half = cols // 2
    rows = ms_hbm.shape[0]
    wrows = w_hbm.shape[0]
    slice_cols = depth // NX
    piece = slice_cols // 2
    total = 4 * tok
    padded = og.shape[0]
    wide = (cols // 256 + 1) // 2 * 256
    narrow = cols - wide
    bh, bw = r1.shape[1], r1.shape[2]
    bwidth = [bw, bw, bw, cols - 3 * bw]

    sister = (group_of(yl, z, 1 - c), l)
    y_near = (group_of(1 - yl, z, c), l)
    y_far = (group_of(1 - yl, z, c), local_of(x, 1 - yh))
    z_up, z_down = (group_of(yl, (z + 1) % NZ, c), l), (group_of(yl, (z + NZ - 1) % NZ, c), l)
    x_up, x_down = (g, local_of((x + 1) % NX, yh)), (g, local_of((x + NX - 1) % NX, yh))

    def send(src, dst, ssem, rsem, device):
        copy = pltpu.make_async_remote_copy(
            src_ref=src, dst_ref=dst, send_sem=ssem, recv_sem=rsem,
            device_id=device, device_id_type=pl.DeviceIdType.MESH,
        )
        copy.start()
        return copy

    def wait_bytes(like, sem):
        pltpu.make_async_copy(like, like, sem).wait()

    def aligned(at, size):
        return pl.ds(pl.multiple_of(at, size), size)

    barrier = pltpu.get_barrier_semaphore()

    @pl.loop(1, NGROUP)
    def _(o):
        pl.semaphore_signal(
            barrier, inc=1, device_id=((g + o) % NGROUP, l), device_id_type=pl.DeviceIdType.MESH
        )

    @pl.loop(2, 2 * NLOCAL)
    def _(o):
        pl.semaphore_signal(
            barrier, inc=1,
            device_id=(group_of((yl + o) % 2, z, c), (l + o // 2) % NLOCAL),
            device_id_type=pl.DeviceIdType.MESH,
        )

    load_x = pltpu.make_async_copy(x_hbm, xs.at[pl.ds(0, tok)], load_sem.at[0])
    load_og = pltpu.make_async_copy(og_hbm, og.at[pl.ds(0, tok)], load_sem.at[1])
    load_ms = pltpu.make_async_copy(ms_hbm, ms, load_sem.at[2])
    load_m1 = pltpu.make_async_copy(m1_hbm, m1, load_sem.at[6])
    load_m2 = pltpu.make_async_copy(m2_hbm, m2, load_sem.at[7])
    load_ms.start()
    load_x.start()
    load_og.start()
    load_m1.start()
    load_m2.start()
    own_w = pltpu.make_async_copy(
        w_hbm.at[:, aligned(l * cols + yl * half, 128 * 7)],
        wt.at[aligned((g * NLOCAL + l) * wrows, wrows)],
        load_sem.at[3],
    )
    own_w.start()

    def own_block(zb, core):
        return aligned((yl * 2 * NZ + zb * 2 + core) * 128, 128)

    @pl.loop(0, NZ)
    def _(zb):
        pltpu.make_async_copy(
            x_hbm.at[:, own_block(zb, c)], xq.at[pl.ds(0, tok), aligned(zb * 128, 128)], load_sem.at[4]
        ).start()

    og[pl.ds(total, padded - total), :] = jnp.zeros((padded - total, cols), BF16)
    xq[pl.ds(total, padded - total), :] = jnp.zeros((padded - total, xq.shape[1]), BF16)
    pl.semaphore_wait(barrier, NGROUP - 1 + 2 * NLOCAL - 2)

    my_rows = aligned((g * NLOCAL + l) * wrows, wrows)

    @pl.loop(1, 2 * NLOCAL)
    def _(o):
        to_l, to_y = (l + o // 2) % NLOCAL, (yl + o) % 2
        send(
            w_hbm.at[:, aligned(to_l * cols + to_y * half, 128 * 7)], wt.at[my_rows],
            aw_sem.at[0], aw_sem.at[1], (group_of(to_y, z, c), to_l),
        )

    def x_columns(side, at, sub, n):
        return aligned(side * (depth // 2) + ((at + NX) % NX) * piece + sub * (piece // 2), n * (piece // 2))

    def far_send(p, side):
        ref = x_hbm.at[:, x_columns(side, x, 0, 2)]
        return send(ref, xs.at[pl.ds(tok, tok), x_columns(side, x, 0, 2)], yo_sem.at[0, p], yo_sem.at[1, p], y_far)

    og_cut = [(0, wide), (wide, narrow)]

    def near_send(p):
        at, n = og_cut[p]
        return send(
            og_hbm.at[:, pl.ds(at, n)], og.at[pl.ds(2 * tok, tok), pl.ds(at, n)],
            yg_sem.at[0, p], yg_sem.at[1, p], y_near,
        )

    far = [far_send(0, 1 - yl)]
    near = [near_send(0)]

    last = g % 4 == 3
    load_ms.wait()
    mb[...] = ms[...].astype(BF16)

    @pl.loop(0, NGROUP // 4)
    def _(q):
        for r in range(4):
            i, n = 4 * q + r, bwidth[r]
            src = mb.at[aligned(q * bh, bh), pl.ds(bw * r, n)]

            @pl.when(g != i)
            def _():
                send(src, r1.at[g, :, pl.ds(0, n)], b1s_sem.at[r // 3], b1r_sem, (i, l))

            @pl.when(g == i)
            def _():
                r1[i, :, pl.ds(0, n)] = src[...]

    far.append(far_send(1, yl))
    near.append(near_send(1))
    og_own = send(og_hbm, og.at[pl.ds(tok, tok)], sg_sem.at[0, 0], sg_sem.at[1, 0], sister)

    @pl.loop(0, NZ)
    def _(zb):
        send(
            x_hbm.at[:, own_block(zb, 1 - c)], xq.at[pl.ds(tok, tok), aligned(zb * 128, 128)],
            sq_sem.at[0, 0], sq_sem.at[1, 0], sister,
        )

    @pl.loop(0, NGROUP)
    def _(j):
        found = jnp.int32(0)
        for i in range(NGROUP):
            found = jnp.where(partner[i] == j, i, found)
        inverse[j] = found

    def by_width(do):
        pl.when(last)(lambda: do(bwidth[3]))
        pl.when(jnp.logical_not(last))(lambda: do(bw))

    def wait_own(ref, sem):
        by_width(lambda n: wait_bytes(ref.at[pl.ds(0, NGROUP - 1), :, pl.ds(0, n)], sem))

    def wait_all(ref, sem):
        full, rest = NGROUP // 4 * 3, NGROUP // 4

        def do(n):
            wait_bytes(ref.at[pl.ds(0, full - (n == bw))], sem.at[0])
            wait_bytes(ref.at[pl.ds(0, rest - (n != bw)), :, pl.ds(0, bwidth[3])], sem.at[1])

        by_width(do)

    def w_block(h, at):
        return wt.at[aligned((h * 2 * NZ + at * 2 + c) * 128, 128)]

    chains = [(0, 1, 0, 4), (1, -1, 1, 4), (2, 1, 1, 3), (3, -1, 0, 3)]
    later = []

    def w_send(k, way, h, s):
        block = w_block(h, (z - way * s + NZ) % NZ)
        copy = send(block, block, ags_sem.at[k, s], agr_sem.at[k, s], z_up if way > 0 else z_down)
        later.append(copy)

    def w_sister(h, at):
        block = w_block(h, at)
        send(block, block, sw_sem.at[0], sw_sem.at[1], sister)

    def w_arrive(s, some):
        for k, way, h, n in chains:
            if k in some and s < n:
                at = (z - way * (s + 1) + NZ) % NZ
                wait_bytes(w_block(h, at), agr_sem.at[k, s])
                if s + 1 < n:
                    w_send(k, way, h, s + 1)
                w_sister(h, at)

    own_w.wait()
    wait_bytes(wt.at[pl.ds(0, 15 * wrows)], aw_sem.at[1])
    for k, way, h, n in chains:
        w_send(k, way, h, 0)
    for h in range(2):
        w_sister(h, z)

    def x_piece(at, p, sub):
        return xs.at[pl.ds(tok, tok), x_columns(yl if p == 0 else 1 - yl, at, sub, 1)]

    def x_send(way, at, p, sub, n):
        ref, sem = x_piece(at, p, sub), xp_sem if way > 0 else xm_sem
        later.append(send(ref, ref, sem.at[0, 3 * p + n], sem.at[1, 3 * p + n], x_up if way > 0 else x_down))

    def x_own(p):
        far[p].wait_recv()
        x_send(1, x, p, 0, 0)
        x_send(-1, x, p, 1, 0)
        x_send(1, x, p, 1, 1)
        x_send(-1, x, p, 0, 1)

    def x_forward(p):
        wait_bytes(x_piece(x, p, 0), xp_sem.at[1, 3 * p])
        x_send(1, x - 1, p, 0, 2)
        wait_bytes(x_piece(x, p, 1), xm_sem.at[1, 3 * p])
        x_send(-1, x + 1, p, 1, 2)

    def x_complete(p):
        for sem in (xp_sem, xm_sem):
            for n in (1, 2):
                wait_bytes(x_piece(x, p, 0), sem.at[1, 3 * p + n])

    def og_forward(p):
        near[p].wait_recv()
        at, n = og_cut[p]
        later.append(
            send(
                og.at[pl.ds(2 * tok, tok), pl.ds(at, n)], og.at[pl.ds(3 * tok, tok), pl.ds(at, n)],
                sg_sem.at[0, 1 + p], sg_sem.at[1, 1 + p], sister,
            )
        )

    def og_arrive(p):
        at, n = og_cut[p]
        wait_bytes(og.at[pl.ds(0, tok), pl.ds(at, n)], sg_sem.at[1, 1 + p])

    early = 2 * tok // 128 * 128

    def turn(at, n):
        @pl.loop(0, NZ)
        def _(zb):
            xt[aligned(zb * 128, 128), pl.ds(at, n)] = xq[pl.ds(at, n), aligned(zb * 128, 128)].T

    def dw_chunk(j):
        at = aligned(j * 256, 256)
        dw[:, at] = jnp.dot(xt[...], og[:, at], preferred_element_type=F32).astype(BF16)

    def dw_block(d, h):
        return dw.at[aligned(((d + 2 * NZ) % NZ) * rows, rows), pl.ds(h * half, half)]

    rs_bufs = [rp0, rm1, rp1, rm0]

    def r_send(k, way, h, n, s):
        src = dw_block(z + way * n, h) if s == 0 else rs_bufs[k].at[s - 1]
        later.append(
            send(src, rs_bufs[k].at[s], rss_sem.at[k, s], rsr_sem.at[k, s], z_up if way > 0 else z_down)
        )

    def r_arrive(s, some):
        for k, way, h, n in chains:
            if k in some and s < n:
                buf = rs_bufs[k]
                wait_bytes(buf.at[s], rsr_sem.at[k, s])
                if s + 1 < n:
                    mine = dw_block(z + way * (n - s - 1), h)
                    buf[s] = (buf[s].astype(F32) + mine[...].astype(F32)).astype(BF16)
                    r_send(k, way, h, n, s + 1)

    def act_chunk(at, n):
        ob[:, pl.ds(at, n)] = jnp.dot(
            xs[...], wt[:, pl.ds(at, n)], preferred_element_type=F32
        ).astype(BF16)

    wait_bytes(xq.at[pl.ds(0, tok)], sq_sem.at[1, 0])
    wait_bytes(xq.at[pl.ds(0, tok)], load_sem.at[4])
    turn(0, early)
    x_own(0)
    w_arrive(0, (0, 1))
    x_forward(0)
    w_arrive(0, (2, 3))
    x_own(1)
    w_arrive(1, (0, 1))
    og_forward(0)
    x_complete(0)

    @pl.loop(0, NZ)
    def _(zb):
        send(
            xs.at[pl.ds(tok, tok), own_block(zb, 1 - c)],
            xq.at[pl.ds(3 * tok, tok), aligned(zb * 128, 128)],
            sq_sem.at[0, 1], sq_sem.at[1, 1], sister,
        )
        pltpu.make_async_copy(
            xs.at[pl.ds(tok, tok), own_block(zb, c)],
            xq.at[pl.ds(2 * tok, tok), aligned(zb * 128, 128)],
            load_sem.at[5],
        ).start()

    w_arrive(1, (2, 3))

    load_og.wait()
    og_own.wait_recv()
    wait_bytes(xq.at[pl.ds(0, tok)], sq_sem.at[1, 1])
    wait_bytes(xq.at[pl.ds(0, tok)], load_sem.at[5])
    turn(early, padded - early)
    w_arrive(2, (0, 1))
    og_arrive(0)
    pl.loop(0, wide // 256)(dw_chunk)
    r_send(0, 1, 0, 4, 0)
    r_send(3, -1, 0, 3, 0)
    x_forward(1)
    og_forward(1)
    w_arrive(2, (2, 3))
    og_arrive(1)
    pl.loop(wide // 256, cols // 256)(dw_chunk)
    r_send(1, -1, 1, 4, 0)
    r_send(2, 1, 1, 3, 0)
    w_arrive(3, (0, 1))

    wait_own(r1, b1r_sem)

    @pl.loop(0, NGROUP)
    def _(j):
        s2[j] = r1[inverse[j]]

    load_x.wait()
    x_complete(1)
    wait_bytes(wt.at[pl.ds(0, depth // 2)], sw_sem.at[1])
    act_chunk(0, 256)
    r_arrive(0, (0, 3))
    act_chunk(256, 256)
    act_chunk(512, 256)
    r_arrive(0, (1, 2))
    act_chunk(768, 128)
    their = send(
        ob.at[pl.ds(tok, tok)], act.at[:, aligned(yl * half, half)], ao_sem.at[0], ao_sem.at[1], y_near
    )
    own_act = pltpu.make_async_copy(
        ob.at[pl.ds(0, tok)], act.at[:, aligned(yl * half, half)], ao_sem.at[2]
    )
    own_act.start()
    r_arrive(1, (0, 3))
    r_arrive(1, (1, 2))
    r_arrive(2, (0, 3))
    r_arrive(2, (1, 2))

    def second_exchange(n):
        @pl.loop(0, NGROUP)
        def _(j):
            @pl.when(g != j)
            def _():
                send(
                    s2.at[j, :, pl.ds(0, n)], b2.at[g, :, pl.ds(0, n)],
                    b2s_sem, b2r_sem.at[0 if n == bw else 1], (j, l),
                )

        b2[g, :, pl.ds(0, n)] = s2[g, :, pl.ds(0, n)]

    by_width(second_exchange)

    r_arrive(3, (0, 1))
    load_m1.wait()
    load_m2.wait()

    @pl.loop(0, rows // bh)
    def _(q):
        at = aligned(q * bh, bh)
        for h, (up, down) in enumerate(((rp0.at[3], rm0.at[2]), (rp1.at[2], rm1.at[3]))):
            here = pl.ds(h * half, half)
            gradient = (
                dw[aligned(z * rows + q * bh, bh), here].astype(F32)
                + up[at, :].astype(F32) + down[at, :].astype(F32)
            )
            one = 0.9 * m1[at, here] + 0.1 * gradient
            two = 0.95 * m2[at, here] + 0.05 * gradient * gradient
            old = ms[at, here]
            new_1[at, here] = one
            new_2[at, here] = two
            new_ms[at, here] = old - 0.0003 * (one / (jnp.sqrt(two) + 1e-08) + 0.1 * old)

    wait_all(b2, b2r_sem)

    @pl.loop(0, NGROUP // 4)
    def _(q):
        for r in range(4):
            bk[aligned(q * bh, bh), pl.ds(bw * r, bwidth[r])] = (
                b2[4 * q + r, :, pl.ds(0, bwidth[r])].astype(F32)
            )

    wait_bytes(wt.at[pl.ds(0, 15 * wrows)], aw_sem.at[0])
    for copy in far + near + later + [og_own]:
        copy.wait_send()
    for n in range(2):
        wait_bytes(xq.at[pl.ds(0, tok)], sq_sem.at[0, n])
    wait_bytes(wt.at[pl.ds(0, depth // 2)], sw_sem.at[0])
    wait_all(r1, b1s_sem)
    wait_own(b2, b2s_sem)
    their.wait()
    own_act.wait()


def exchange(partner, inputs, weight, out_grad, master, moment_one, moment_two):
    tok, depth = inputs.shape
    cols = out_grad.shape[1]
    rows = master.shape[0]
    padded = -(-4 * tok // 256) * 256
    half = cols // 2
    dma = pltpu.SemaphoreType.DMA
    hbm = pl.BlockSpec(memory_space=pl.ANY)
    vmem = pl.BlockSpec(memory_space=pltpu.VMEM)
    return pl.pallas_call(
        kernel,
        out_shape=(pltpu.VMEM((tok, cols), BF16),) + (pltpu.VMEM((rows, cols), F32),) * 4,
        in_specs=[pl.BlockSpec(memory_space=pltpu.SMEM)] + [hbm] * 6,
        out_specs=(vmem,) * 5,
        scratch_shapes=[
            pltpu.VMEM((2 * tok, depth), BF16),
            pltpu.VMEM((depth, half), BF16),
            pltpu.VMEM((padded, NZ * rows), BF16),
            pltpu.VMEM((NZ * rows, padded), BF16),
            pltpu.VMEM((padded, cols), BF16),
            pltpu.VMEM((NZ * rows, cols), BF16),
            pltpu.VMEM((4, rows, half), BF16),
            pltpu.VMEM((3, rows, half), BF16),
            pltpu.VMEM((3, rows, half), BF16),
            pltpu.VMEM((4, rows, half), BF16),
            pltpu.VMEM((2 * tok, half), BF16),
            pltpu.VMEM((rows, cols), F32),
            pltpu.VMEM((rows, cols), F32),
            pltpu.VMEM((rows, cols), F32),
            pltpu.VMEM((rows, cols), BF16),
            pltpu.VMEM((NGROUP, rows // 8, 512), BF16),
            pltpu.VMEM((NGROUP, rows // 8, 512), BF16),
            pltpu.VMEM((NGROUP, rows // 8, 512), BF16),
            pltpu.SMEM((NGROUP,), jnp.int32),
            dma((8,)), dma((2,)), dma((2, 2)), dma((2, 6)), dma((2, 6)), dma((2, 2)), dma((2, 3)), dma((2, 2)),
            dma((4, 4)), dma((4, 4)), dma((2,)), dma((4, 4)), dma((4, 4)), dma((3,)), dma, dma((2,)), dma((2,)), dma,
        ],
        compiler_params=pltpu.CompilerParams(
            collective_id=0, has_side_effects=True, vmem_limit_bytes=50 * 2**20
        ),
    )(partner, inputs, weight, out_grad, master, moment_one, moment_two)


def store(*refs):
    count = len(refs) // 2
    copies = [pltpu.make_async_copy(refs[i], refs[count + i], refs[-1].at[i]) for i in range(count)]
    for copy in copies:
        copy.start()
    for copy in copies:
        copy.wait()


def on_device(inputs, weight, out_grad, master, moment_one, moment_two, partner):
    results = exchange(partner, inputs, weight, out_grad, master, moment_one, moment_two)
    return pl.pallas_call(
        store,
        out_shape=tuple(jax.ShapeDtypeStruct(r.shape, r.dtype) for r in results),
        in_specs=[pl.BlockSpec(memory_space=pltpu.VMEM)] * len(results),
        out_specs=(pl.BlockSpec(memory_space=pl.ANY),) * len(results),
        scratch_shapes=[pltpu.SemaphoreType.DMA((len(results),))],
    )(*results)


def solution(mesh):
    split = P("group", "local")
    return jax.shard_map(
        on_device,
        mesh=mesh,
        in_specs=(P("group", None), P(("group", "local"), None), split, split, split, split, P()),
        out_specs=(split,) * 5,
        check_vma=False,
    )
```

```python
import jax
import jax.numpy as jnp
from jax import lax
from jax.experimental import pallas as pl
from jax.experimental.pallas import tpu as pltpu
from jax.sharding import PartitionSpec as P

NZ = 8
NX = 4
NLOCAL = 8
NGROUP = 32
BF16 = jnp.bfloat16
F32 = jnp.float32


def group_of(yl, z, c):
    return (yl * NZ + z) * 2 + c


def local_of(x, yh):
    return x * 2 + yh


def kernel(
    partner, x_hbm, w_hbm, og_hbm, ms_hbm, m1_hbm, m2_hbm,
    act, new_ms, new_1, new_2, bk,
    xs, wt, xq, xt, og, dw, rp0, rp1, rm0, rm1, ob, ms, m1, m2, mb, r1, s2, b2,
    inverse, load_sem, aw_sem, yo_sem, xp_sem, xm_sem, yg_sem, sg_sem, sq_sem,
    agr_sem, ags_sem, sw_sem, rsr_sem, rss_sem, ao_sem, b1r_sem, b1s_sem, b2r_sem, b2s_sem,
):
    g, l = lax.axis_index("group"), lax.axis_index("local")
    yl, z, c = g // (2 * NZ), (g // 2) % NZ, g % 2
    x, yh = l // 2, l % 2
    tok, depth = x_hbm.shape
    cols = og_hbm.shape[1]
    half = cols // 2
    rows = ms_hbm.shape[0]
    wrows = w_hbm.shape[0]
    slice_cols = depth // NX
    piece = slice_cols // 2
    total = 4 * tok
    padded = og.shape[0]
    wide = (cols // 256 + 1) // 2 * 256
    narrow = cols - wide
    bh, bw = r1.shape[1], r1.shape[2]
    bwidth = [bw, bw, bw, cols - 3 * bw]

    sister = (group_of(yl, z, 1 - c), l)
    y_near = (group_of(1 - yl, z, c), l)
    y_far = (group_of(1 - yl, z, c), local_of(x, 1 - yh))
    z_up, z_down = (group_of(yl, (z + 1) % NZ, c), l), (group_of(yl, (z + NZ - 1) % NZ, c), l)
    x_up, x_down = (g, local_of((x + 1) % NX, yh)), (g, local_of((x + NX - 1) % NX, yh))

    def send(src, dst, ssem, rsem, device):
        copy = pltpu.make_async_remote_copy(
            src_ref=src, dst_ref=dst, send_sem=ssem, recv_sem=rsem,
            device_id=device, device_id_type=pl.DeviceIdType.MESH,
        )
        copy.start()
        return copy

    def wait_bytes(like, sem):
        pltpu.make_async_copy(like, like, sem).wait()

    def aligned(at, size):
        return pl.ds(pl.multiple_of(at, size), size)

    barrier = pltpu.get_barrier_semaphore()

    @pl.loop(1, NGROUP)
    def _(o):
        pl.semaphore_signal(
            barrier, inc=1, device_id=((g + o) % NGROUP, l), device_id_type=pl.DeviceIdType.MESH
        )

    @pl.loop(2, 2 * NLOCAL)
    def _(o):
        pl.semaphore_signal(
            barrier, inc=1,
            device_id=(group_of((yl + o) % 2, z, c), (l + o // 2) % NLOCAL),
            device_id_type=pl.DeviceIdType.MESH,
        )

    load_x = pltpu.make_async_copy(x_hbm, xs.at[pl.ds(0, tok)], load_sem.at[0])
    load_og = pltpu.make_async_copy(og_hbm, og.at[pl.ds(0, tok)], load_sem.at[1])
    load_ms = pltpu.make_async_copy(ms_hbm, ms, load_sem.at[2])
    load_m1 = pltpu.make_async_copy(m1_hbm, m1, load_sem.at[6])
    load_m2 = pltpu.make_async_copy(m2_hbm, m2, load_sem.at[7])
    load_ms.start()
    load_x.start()
    load_og.start()
    load_m1.start()
    load_m2.start()
    own_w = pltpu.make_async_copy(
        w_hbm.at[:, aligned(l * cols + yl * half, 128 * 7)],
        wt.at[aligned((g * NLOCAL + l) * wrows, wrows)],
        load_sem.at[3],
    )
    own_w.start()

    def own_block(zb, core):
        return aligned((yl * 2 * NZ + zb * 2 + core) * 128, 128)

    @pl.loop(0, NZ)
    def _(zb):
        pltpu.make_async_copy(
            x_hbm.at[:, own_block(zb, c)], xq.at[pl.ds(0, tok), aligned(zb * 128, 128)], load_sem.at[4]
        ).start()

    og[pl.ds(total, padded - total), :] = jnp.zeros((padded - total, cols), BF16)
    xq[pl.ds(total, padded - total), :] = jnp.zeros((padded - total, xq.shape[1]), BF16)
    pl.semaphore_wait(barrier, NGROUP - 1 + 2 * NLOCAL - 2)

    my_rows = aligned((g * NLOCAL + l) * wrows, wrows)

    @pl.loop(1, 2 * NLOCAL)
    def _(o):
        to_l, to_y = (l + o // 2) % NLOCAL, (yl + o) % 2
        send(
            w_hbm.at[:, aligned(to_l * cols + to_y * half, 128 * 7)], wt.at[my_rows],
            aw_sem.at[0], aw_sem.at[1], (group_of(to_y, z, c), to_l),
        )

    def x_columns(side, at, sub, n):
        return aligned(side * (depth // 2) + ((at + NX) % NX) * piece + sub * (piece // 2), n * (piece // 2))

    def far_send(p, side):
        ref = x_hbm.at[:, x_columns(side, x, 0, 2)]
        return send(ref, xs.at[pl.ds(tok, tok), x_columns(side, x, 0, 2)], yo_sem.at[0, p], yo_sem.at[1, p], y_far)

    og_cut = [(0, wide), (wide, narrow)]

    def near_send(p):
        at, n = og_cut[p]
        return send(
            og_hbm.at[:, pl.ds(at, n)], og.at[pl.ds(2 * tok, tok), pl.ds(at, n)],
            yg_sem.at[0, p], yg_sem.at[1, p], y_near,
        )

    far = [far_send(0, 1 - yl)]
    near = [near_send(0)]

    last = g % 4 == 3
    load_ms.wait()
    mb[...] = ms[...].astype(BF16)

    @pl.loop(0, NGROUP // 4)
    def _(q):
        for r in range(4):
            i, n = 4 * q + r, bwidth[r]
            src = mb.at[aligned(q * bh, bh), pl.ds(bw * r, n)]

            @pl.when(g != i)
            def _():
                send(src, r1.at[g, :, pl.ds(0, n)], b1s_sem.at[r // 3], b1r_sem, (i, l))

            @pl.when(g == i)
            def _():
                r1[i, :, pl.ds(0, n)] = src[...]

    far.append(far_send(1, yl))
    near.append(near_send(1))
    og_own = send(og_hbm, og.at[pl.ds(tok, tok)], sg_sem.at[0, 0], sg_sem.at[1, 0], sister)

    @pl.loop(0, NZ)
    def _(zb):
        send(
            x_hbm.at[:, own_block(zb, 1 - c)], xq.at[pl.ds(tok, tok), aligned(zb * 128, 128)],
            sq_sem.at[0, 0], sq_sem.at[1, 0], sister,
        )

    @pl.loop(0, NGROUP)
    def _(j):
        found = jnp.int32(0)
        for i in range(NGROUP):
            found = jnp.where(partner[i] == j, i, found)
        inverse[j] = found

    def by_width(do):
        pl.when(last)(lambda: do(bwidth[3]))
        pl.when(jnp.logical_not(last))(lambda: do(bw))

    def wait_own(ref, sem):
        by_width(lambda n: wait_bytes(ref.at[pl.ds(0, NGROUP - 1), :, pl.ds(0, n)], sem))

    def wait_all(ref, sem):
        full, rest = NGROUP // 4 * 3, NGROUP // 4

        def do(n):
            wait_bytes(ref.at[pl.ds(0, full - (n == bw))], sem.at[0])
            wait_bytes(ref.at[pl.ds(0, rest - (n != bw)), :, pl.ds(0, bwidth[3])], sem.at[1])

        by_width(do)

    def w_block(h, at):
        return wt.at[aligned((h * 2 * NZ + at * 2 + c) * 128, 128)]

    chains = [(0, 1, 0, 4), (1, -1, 1, 4), (2, 1, 1, 3), (3, -1, 0, 3)]
    later = []

    def w_send(k, way, h, s):
        block = w_block(h, (z - way * s + NZ) % NZ)
        copy = send(block, block, ags_sem.at[k, s], agr_sem.at[k, s], z_up if way > 0 else z_down)
        later.append(copy)

    def w_sister(h, at):
        block = w_block(h, at)
        send(block, block, sw_sem.at[0], sw_sem.at[1], sister)

    def w_arrive(s, some):
        for k, way, h, n in chains:
            if k in some and s < n:
                at = (z - way * (s + 1) + NZ) % NZ
                wait_bytes(w_block(h, at), agr_sem.at[k, s])
                if s + 1 < n:
                    w_send(k, way, h, s + 1)
                w_sister(h, at)

    own_w.wait()
    wait_bytes(wt.at[pl.ds(0, 15 * wrows)], aw_sem.at[1])
    for k, way, h, n in chains:
        w_send(k, way, h, 0)
    for h in range(2):
        w_sister(h, z)

    def x_piece(at, p, sub):
        return xs.at[pl.ds(tok, tok), x_columns(yl if p == 0 else 1 - yl, at, sub, 1)]

    def x_send(way, at, p, sub, n):
        ref, sem = x_piece(at, p, sub), xp_sem if way > 0 else xm_sem
        later.append(send(ref, ref, sem.at[0, 3 * p + n], sem.at[1, 3 * p + n], x_up if way > 0 else x_down))

    def x_own(p):
        far[p].wait_recv()
        x_send(1, x, p, 0, 0)
        x_send(-1, x, p, 1, 0)
        x_send(1, x, p, 1, 1)
        x_send(-1, x, p, 0, 1)

    def x_forward(p):
        wait_bytes(x_piece(x, p, 0), xp_sem.at[1, 3 * p])
        x_send(1, x - 1, p, 0, 2)
        wait_bytes(x_piece(x, p, 1), xm_sem.at[1, 3 * p])
        x_send(-1, x + 1, p, 1, 2)

    def x_complete(p):
        for sem in (xp_sem, xm_sem):
            for n in (1, 2):
                wait_bytes(x_piece(x, p, 0), sem.at[1, 3 * p + n])

    def og_forward(p):
        near[p].wait_recv()
        at, n = og_cut[p]
        later.append(
            send(
                og.at[pl.ds(2 * tok, tok), pl.ds(at, n)], og.at[pl.ds(3 * tok, tok), pl.ds(at, n)],
                sg_sem.at[0, 1 + p], sg_sem.at[1, 1 + p], sister,
            )
        )

    def og_arrive(p):
        at, n = og_cut[p]
        wait_bytes(og.at[pl.ds(0, tok), pl.ds(at, n)], sg_sem.at[1, 1 + p])

    early = 2 * tok // 128 * 128

    def turn(at, n):
        @pl.loop(0, NZ)
        def _(zb):
            xt[aligned(zb * 128, 128), pl.ds(at, n)] = xq[pl.ds(at, n), aligned(zb * 128, 128)].T

    def dw_chunk(j):
        at = aligned(j * 256, 256)
        dw[:, at] = jnp.dot(xt[...], og[:, at], preferred_element_type=F32).astype(BF16)

    def dw_block(d, h):
        return dw.at[aligned(((d + 2 * NZ) % NZ) * rows, rows), pl.ds(h * half, half)]

    rs_bufs = [rp0, rm1, rp1, rm0]

    def r_send(k, way, h, n, s):
        src = dw_block(z + way * n, h) if s == 0 else rs_bufs[k].at[s - 1]
        later.append(
            send(src, rs_bufs[k].at[s], rss_sem.at[k, s], rsr_sem.at[k, s], z_up if way > 0 else z_down)
        )

    def r_arrive(s, some):
        for k, way, h, n in chains:
            if k in some and s < n:
                buf = rs_bufs[k]
                wait_bytes(buf.at[s], rsr_sem.at[k, s])
                if s + 1 < n:
                    mine = dw_block(z + way * (n - s - 1), h)
                    buf[s] = (buf[s].astype(F32) + mine[...].astype(F32)).astype(BF16)
                    r_send(k, way, h, n, s + 1)

    def act_chunk(at, n):
        ob[:, pl.ds(at, n)] = jnp.dot(
            xs[...], wt[:, pl.ds(at, n)], preferred_element_type=F32
        ).astype(BF16)

    wait_bytes(xq.at[pl.ds(0, tok)], sq_sem.at[1, 0])
    wait_bytes(xq.at[pl.ds(0, tok)], load_sem.at[4])
    turn(0, early)
    x_own(0)
    w_arrive(0, (0, 1))
    x_forward(0)
    w_arrive(0, (2, 3))
    x_own(1)
    w_arrive(1, (0, 1))
    og_forward(0)
    x_complete(0)

    @pl.loop(0, NZ)
    def _(zb):
        send(
            xs.at[pl.ds(tok, tok), own_block(zb, 1 - c)],
            xq.at[pl.ds(3 * tok, tok), aligned(zb * 128, 128)],
            sq_sem.at[0, 1], sq_sem.at[1, 1], sister,
        )
        pltpu.make_async_copy(
            xs.at[pl.ds(tok, tok), own_block(zb, c)],
            xq.at[pl.ds(2 * tok, tok), aligned(zb * 128, 128)],
            load_sem.at[5],
        ).start()

    w_arrive(1, (2, 3))

    load_og.wait()
    og_own.wait_recv()
    wait_bytes(xq.at[pl.ds(0, tok)], sq_sem.at[1, 1])
    wait_bytes(xq.at[pl.ds(0, tok)], load_sem.at[5])
    turn(early, padded - early)
    w_arrive(2, (0, 1))
    og_arrive(0)
    pl.loop(0, wide // 256)(dw_chunk)
    r_send(0, 1, 0, 4, 0)
    r_send(3, -1, 0, 3, 0)
    x_forward(1)
    og_forward(1)
    w_arrive(2, (2, 3))
    og_arrive(1)
    pl.loop(wide // 256, cols // 256)(dw_chunk)
    r_send(1, -1, 1, 4, 0)
    r_send(2, 1, 1, 3, 0)
    w_arrive(3, (0, 1))

    wait_own(r1, b1r_sem)

    @pl.loop(0, NGROUP)
    def _(j):
        s2[j] = r1[inverse[j]]

    load_x.wait()
    x_complete(1)
    wait_bytes(wt.at[pl.ds(0, depth // 2)], sw_sem.at[1])
    act_chunk(0, 256)
    r_arrive(0, (0, 3))
    act_chunk(256, 256)
    act_chunk(512, 256)
    r_arrive(0, (1, 2))
    act_chunk(768, 128)
    their = send(
        ob.at[pl.ds(tok, tok)], act.at[:, aligned(yl * half, half)], ao_sem.at[0], ao_sem.at[1], y_near
    )
    own_act = pltpu.make_async_copy(
        ob.at[pl.ds(0, tok)], act.at[:, aligned(yl * half, half)], ao_sem.at[2]
    )
    own_act.start()
    r_arrive(1, (0, 3))
    r_arrive(1, (1, 2))
    r_arrive(2, (0, 3))
    r_arrive(2, (1, 2))

    def second_exchange(n):
        @pl.loop(0, NGROUP)
        def _(j):
            @pl.when(g != j)
            def _():
                send(
                    s2.at[j, :, pl.ds(0, n)], b2.at[g, :, pl.ds(0, n)],
                    b2s_sem, b2r_sem.at[0 if n == bw else 1], (j, l),
                )

        b2[g, :, pl.ds(0, n)] = s2[g, :, pl.ds(0, n)]

    by_width(second_exchange)

    r_arrive(3, (0, 1))
    load_m1.wait()
    load_m2.wait()

    @pl.loop(0, rows // bh)
    def _(q):
        at = aligned(q * bh, bh)
        for h, (up, down) in enumerate(((rp0.at[3], rm0.at[2]), (rp1.at[2], rm1.at[3]))):
            here = pl.ds(h * half, half)
            gradient = (
                dw[aligned(z * rows + q * bh, bh), here].astype(F32)
                + up[at, :].astype(F32) + down[at, :].astype(F32)
            )
            one = 0.9 * m1[at, here] + 0.1 * gradient
            two = 0.95 * m2[at, here] + 0.05 * gradient * gradient
            old = ms[at, here]
            new_1[at, here] = one
            new_2[at, here] = two
            new_ms[at, here] = old - 0.0003 * (one / (jnp.sqrt(two) + 1e-08) + 0.1 * old)

    wait_all(b2, b2r_sem)

    @pl.loop(0, NGROUP // 4)
    def _(q):
        for r in range(4):
            bk[aligned(q * bh, bh), pl.ds(bw * r, bwidth[r])] = (
                b2[4 * q + r, :, pl.ds(0, bwidth[r])].astype(F32)
            )

    wait_bytes(wt.at[pl.ds(0, 15 * wrows)], aw_sem.at[0])
    for copy in far + near + later + [og_own]:
        copy.wait_send()
    for n in range(2):
        wait_bytes(xq.at[pl.ds(0, tok)], sq_sem.at[0, n])
    wait_bytes(wt.at[pl.ds(0, depth // 2)], sw_sem.at[0])
    wait_all(r1, b1s_sem)
    wait_own(b2, b2s_sem)
    their.wait()
    own_act.wait()


def exchange(partner, inputs, weight, out_grad, master, moment_one, moment_two):
    tok, depth = inputs.shape
    cols = out_grad.shape[1]
    rows = master.shape[0]
    padded = -(-4 * tok // 256) * 256
    half = cols // 2
    dma = pltpu.SemaphoreType.DMA
    hbm = pl.BlockSpec(memory_space=pl.ANY)
    vmem = pl.BlockSpec(memory_space=pltpu.VMEM)
    return pl.pallas_call(
        kernel,
        out_shape=(pltpu.VMEM((tok, cols), BF16),) + (pltpu.VMEM((rows, cols), F32),) * 4,
        in_specs=[pl.BlockSpec(memory_space=pltpu.SMEM)] + [hbm] * 6,
        out_specs=(vmem,) * 5,
        scratch_shapes=[
            pltpu.VMEM((2 * tok, depth), BF16),
            pltpu.VMEM((depth, half), BF16),
            pltpu.VMEM((padded, NZ * rows), BF16),
            pltpu.VMEM((NZ * rows, padded), BF16),
            pltpu.VMEM((padded, cols), BF16),
            pltpu.VMEM((NZ * rows, cols), BF16),
            pltpu.VMEM((4, rows, half), BF16),
            pltpu.VMEM((3, rows, half), BF16),
            pltpu.VMEM((3, rows, half), BF16),
            pltpu.VMEM((4, rows, half), BF16),
            pltpu.VMEM((2 * tok, half), BF16),
            pltpu.VMEM((rows, cols), F32),
            pltpu.VMEM((rows, cols), F32),
            pltpu.VMEM((rows, cols), F32),
            pltpu.VMEM((rows, cols), BF16),
            pltpu.VMEM((NGROUP, rows // 8, 512), BF16),
            pltpu.VMEM((NGROUP, rows // 8, 512), BF16),
            pltpu.VMEM((NGROUP, rows // 8, 512), BF16),
            pltpu.SMEM((NGROUP,), jnp.int32),
            dma((8,)), dma((2,)), dma((2, 2)), dma((2, 6)), dma((2, 6)), dma((2, 2)), dma((2, 3)), dma((2, 2)),
            dma((4, 4)), dma((4, 4)), dma((2,)), dma((4, 4)), dma((4, 4)), dma((3,)), dma, dma((2,)), dma((2,)), dma,
        ],
        compiler_params=pltpu.CompilerParams(
            collective_id=0, has_side_effects=True, vmem_limit_bytes=50 * 2**20
        ),
    )(partner, inputs, weight, out_grad, master, moment_one, moment_two)


def store(*refs):
    count = len(refs) // 2
    copies = [pltpu.make_async_copy(refs[i], refs[count + i], refs[-1].at[i]) for i in range(count)]
    for copy in copies:
        copy.start()
    for copy in copies:
        copy.wait()


def on_device(inputs, weight, out_grad, master, moment_one, moment_two, partner):
    results = exchange(partner, inputs, weight, out_grad, master, moment_one, moment_two)
    return pl.pallas_call(
        store,
        out_shape=tuple(jax.ShapeDtypeStruct(r.shape, r.dtype) for r in results),
        in_specs=[pl.BlockSpec(memory_space=pl.ANY)] * len(results),
        out_specs=(pl.BlockSpec(memory_space=pl.ANY),) * len(results),
        scratch_shapes=[pltpu.SemaphoreType.DMA((len(results),))],
        compiler_params=pltpu.CompilerParams(vmem_limit_bytes=8 * 2**20),
    )(*results)


def solution(mesh):
    split = P("group", "local")
    return jax.shard_map(
        on_device,
        mesh=mesh,
        in_specs=(P("group", None), P(("group", "local"), None), split, split, split, split, P()),
        out_specs=(split,) * 5,
        check_vma=False,
    )
```

```python
import jax
import jax.numpy as jnp
from jax import lax
from jax.experimental import pallas as pl
from jax.experimental.pallas import tpu as pltpu
from jax.sharding import PartitionSpec as P

NZ = 8
NX = 4
NLOCAL = 8
NGROUP = 32
BF16 = jnp.bfloat16
F32 = jnp.float32


def group_of(yl, z, c):
    return (yl * NZ + z) * 2 + c


def local_of(x, yh):
    return x * 2 + yh


def kernel(
    partner, x_hbm, w_hbm, og_hbm, ms_hbm, m1_hbm, m2_hbm,
    act, new_ms, new_1, new_2, bk,
    xs, wt, xq, xt, og, dw, rp0, rp1, rm0, rm1, ob, ms, m1, m2, mb, r1, s2, b2,
    inverse, load_sem, aw_sem, yo_sem, xp_sem, xm_sem, yg_sem, sg_sem, sq_sem,
    agr_sem, ags_sem, sw_sem, rsr_sem, rss_sem, ao_sem, b1r_sem, b1s_sem, b2r_sem, b2s_sem,
):
    g, l = lax.axis_index("group"), lax.axis_index("local")
    yl, z, c = g // (2 * NZ), (g // 2) % NZ, g % 2
    x, yh = l // 2, l % 2
    tok, depth = x_hbm.shape
    cols = og_hbm.shape[1]
    half = cols // 2
    rows = ms_hbm.shape[0]
    wrows = w_hbm.shape[0]
    slice_cols = depth // NX
    piece = slice_cols // 2
    total = 4 * tok
    padded = og.shape[0]
    wide = (cols // 256 + 1) // 2 * 256
    narrow = cols - wide
    bh, bw = r1.shape[1], r1.shape[2]
    bwidth = [bw, bw, bw, cols - 3 * bw]

    sister = (group_of(yl, z, 1 - c), l)
    y_near = (group_of(1 - yl, z, c), l)
    y_far = (group_of(1 - yl, z, c), local_of(x, 1 - yh))
    z_up, z_down = (group_of(yl, (z + 1) % NZ, c), l), (group_of(yl, (z + NZ - 1) % NZ, c), l)
    x_up, x_down = (g, local_of((x + 1) % NX, yh)), (g, local_of((x + NX - 1) % NX, yh))

    def send(src, dst, ssem, rsem, device):
        copy = pltpu.make_async_remote_copy(
            src_ref=src, dst_ref=dst, send_sem=ssem, recv_sem=rsem,
            device_id=device, device_id_type=pl.DeviceIdType.MESH,
        )
        copy.start()
        return copy

    def wait_bytes(like, sem):
        pltpu.make_async_copy(like, like, sem).wait()

    def aligned(at, size):
        return pl.ds(pl.multiple_of(at, size), size)

    barrier = pltpu.get_barrier_semaphore()

    @pl.loop(1, NGROUP)
    def _(o):
        pl.semaphore_signal(
            barrier, inc=1, device_id=((g + o) % NGROUP, l), device_id_type=pl.DeviceIdType.MESH
        )

    @pl.loop(2, 2 * NLOCAL)
    def _(o):
        pl.semaphore_signal(
            barrier, inc=1,
            device_id=(group_of((yl + o) % 2, z, c), (l + o // 2) % NLOCAL),
            device_id_type=pl.DeviceIdType.MESH,
        )

    load_x = pltpu.make_async_copy(x_hbm, xs.at[pl.ds(0, tok)], load_sem.at[0])
    load_og = pltpu.make_async_copy(og_hbm, og.at[pl.ds(0, tok)], load_sem.at[1])
    load_ms = pltpu.make_async_copy(ms_hbm, ms, load_sem.at[2])
    load_m1 = pltpu.make_async_copy(m1_hbm, m1, load_sem.at[6])
    load_m2 = pltpu.make_async_copy(m2_hbm, m2, load_sem.at[7])
    load_ms.start()
    own_w = pltpu.make_async_copy(
        w_hbm.at[:, aligned(l * cols + yl * half, 128 * 7)],
        wt.at[aligned((g * NLOCAL + l) * wrows, wrows)],
        load_sem.at[3],
    )
    own_w.start()

    def own_block(zb, core):
        return aligned((yl * 2 * NZ + zb * 2 + core) * 128, 128)

    pl.semaphore_wait(barrier, NGROUP - 1 + 2 * NLOCAL - 2)

    my_rows = aligned((g * NLOCAL + l) * wrows, wrows)

    @pl.loop(1, 2 * NLOCAL)
    def _(o):
        to_l, to_y = (l + o // 2) % NLOCAL, (yl + o) % 2
        send(
            w_hbm.at[:, aligned(to_l * cols + to_y * half, 128 * 7)], wt.at[my_rows],
            aw_sem.at[0], aw_sem.at[1], (group_of(to_y, z, c), to_l),
        )

    def x_columns(side, at, sub, n):
        return aligned(side * (depth // 2) + ((at + NX) % NX) * piece + sub * (piece // 2), n * (piece // 2))

    def far_send(p, side):
        ref = x_hbm.at[:, x_columns(side, x, 0, 2)]
        return send(ref, xs.at[pl.ds(tok, tok), x_columns(side, x, 0, 2)], yo_sem.at[0, p], yo_sem.at[1, p], y_far)

    og_cut = [(0, wide), (wide, narrow)]

    def near_send(p):
        at, n = og_cut[p]
        return send(
            og_hbm.at[:, pl.ds(at, n)], og.at[pl.ds(2 * tok, tok), pl.ds(at, n)],
            yg_sem.at[0, p], yg_sem.at[1, p], y_near,
        )

    far = [far_send(0, 1 - yl)]
    near = [near_send(0)]

    last = g % 4 == 3
    load_ms.wait()
    mb[...] = ms[...].astype(BF16)

    @pl.loop(0, NGROUP // 4)
    def _(q):
        for r in range(4):
            i, n = 4 * q + r, bwidth[r]
            src = mb.at[aligned(q * bh, bh), pl.ds(bw * r, n)]

            @pl.when(g != i)
            def _():
                send(src, r1.at[g, :, pl.ds(0, n)], b1s_sem.at[r // 3], b1r_sem, (i, l))

            @pl.when(g == i)
            def _():
                r1[i, :, pl.ds(0, n)] = src[...]

    far.append(far_send(1, yl))
    near.append(near_send(1))
    og_own = send(og_hbm, og.at[pl.ds(tok, tok)], sg_sem.at[0, 0], sg_sem.at[1, 0], sister)
    load_x.start()
    load_og.start()
    load_m1.start()
    load_m2.start()

    @pl.loop(0, NZ)
    def _(zb):
        pltpu.make_async_copy(
            x_hbm.at[:, own_block(zb, c)], xq.at[pl.ds(0, tok), aligned(zb * 128, 128)], load_sem.at[4]
        ).start()

    og[pl.ds(total, padded - total), :] = jnp.zeros((padded - total, cols), BF16)
    xq[pl.ds(total, padded - total), :] = jnp.zeros((padded - total, xq.shape[1]), BF16)

    @pl.loop(0, NZ)
    def _(zb):
        send(
            x_hbm.at[:, own_block(zb, 1 - c)], xq.at[pl.ds(tok, tok), aligned(zb * 128, 128)],
            sq_sem.at[0, 0], sq_sem.at[1, 0], sister,
        )

    @pl.loop(0, NGROUP)
    def _(j):
        found = jnp.int32(0)
        for i in range(NGROUP):
            found = jnp.where(partner[i] == j, i, found)
        inverse[j] = found

    def by_width(do):
        pl.when(last)(lambda: do(bwidth[3]))
        pl.when(jnp.logical_not(last))(lambda: do(bw))

    def wait_own(ref, sem):
        by_width(lambda n: wait_bytes(ref.at[pl.ds(0, NGROUP - 1), :, pl.ds(0, n)], sem))

    def wait_all(ref, sem):
        full, rest = NGROUP // 4 * 3, NGROUP // 4

        def do(n):
            wait_bytes(ref.at[pl.ds(0, full - (n == bw))], sem.at[0])
            wait_bytes(ref.at[pl.ds(0, rest - (n != bw)), :, pl.ds(0, bwidth[3])], sem.at[1])

        by_width(do)

    def w_block(h, at):
        return wt.at[aligned((h * 2 * NZ + at * 2 + c) * 128, 128)]

    chains = [(0, 1, 0, 4), (1, -1, 1, 4), (2, 1, 1, 3), (3, -1, 0, 3)]
    later = []

    def w_send(k, way, h, s):
        block = w_block(h, (z - way * s + NZ) % NZ)
        copy = send(block, block, ags_sem.at[k, s], agr_sem.at[k, s], z_up if way > 0 else z_down)
        later.append(copy)

    def w_sister(h, at):
        block = w_block(h, at)
        send(block, block, sw_sem.at[0], sw_sem.at[1], sister)

    def w_arrive(s, some):
        for k, way, h, n in chains:
            if k in some and s < n:
                at = (z - way * (s + 1) + NZ) % NZ
                wait_bytes(w_block(h, at), agr_sem.at[k, s])
                if s + 1 < n:
                    w_send(k, way, h, s + 1)
                w_sister(h, at)

    own_w.wait()
    wait_bytes(wt.at[pl.ds(0, 15 * wrows)], aw_sem.at[1])
    for k, way, h, n in chains:
        w_send(k, way, h, 0)
    for h in range(2):
        w_sister(h, z)

    def x_piece(at, p, sub):
        return xs.at[pl.ds(tok, tok), x_columns(yl if p == 0 else 1 - yl, at, sub, 1)]

    def x_send(way, at, p, sub, n):
        ref, sem = x_piece(at, p, sub), xp_sem if way > 0 else xm_sem
        later.append(send(ref, ref, sem.at[0, 3 * p + n], sem.at[1, 3 * p + n], x_up if way > 0 else x_down))

    def x_own(p):
        far[p].wait_recv()
        x_send(1, x, p, 0, 0)
        x_send(-1, x, p, 1, 0)
        x_send(1, x, p, 1, 1)
        x_send(-1, x, p, 0, 1)

    def x_forward(p):
        wait_bytes(x_piece(x, p, 0), xp_sem.at[1, 3 * p])
        x_send(1, x - 1, p, 0, 2)
        wait_bytes(x_piece(x, p, 1), xm_sem.at[1, 3 * p])
        x_send(-1, x + 1, p, 1, 2)

    def x_complete(p):
        for sem in (xp_sem, xm_sem):
            for n in (1, 2):
                wait_bytes(x_piece(x, p, 0), sem.at[1, 3 * p + n])

    def og_forward(p):
        near[p].wait_recv()
        at, n = og_cut[p]
        later.append(
            send(
                og.at[pl.ds(2 * tok, tok), pl.ds(at, n)], og.at[pl.ds(3 * tok, tok), pl.ds(at, n)],
                sg_sem.at[0, 1 + p], sg_sem.at[1, 1 + p], sister,
            )
        )

    def og_arrive(p):
        at, n = og_cut[p]
        wait_bytes(og.at[pl.ds(0, tok), pl.ds(at, n)], sg_sem.at[1, 1 + p])

    early = 2 * tok // 128 * 128

    def turn(at, n):
        @pl.loop(0, NZ)
        def _(zb):
            xt[aligned(zb * 128, 128), pl.ds(at, n)] = xq[pl.ds(at, n), aligned(zb * 128, 128)].T

    def dw_chunk(j):
        at = aligned(j * 256, 256)
        dw[:, at] = jnp.dot(xt[...], og[:, at], preferred_element_type=F32).astype(BF16)

    def dw_block(d, h):
        return dw.at[aligned(((d + 2 * NZ) % NZ) * rows, rows), pl.ds(h * half, half)]

    rs_bufs = [rp0, rm1, rp1, rm0]

    def r_send(k, way, h, n, s):
        src = dw_block(z + way * n, h) if s == 0 else rs_bufs[k].at[s - 1]
        later.append(
            send(src, rs_bufs[k].at[s], rss_sem.at[k, s], rsr_sem.at[k, s], z_up if way > 0 else z_down)
        )

    def r_arrive(s, some):
        for k, way, h, n in chains:
            if k in some and s < n:
                buf = rs_bufs[k]
                wait_bytes(buf.at[s], rsr_sem.at[k, s])
                if s + 1 < n:
                    mine = dw_block(z + way * (n - s - 1), h)
                    buf[s] = (buf[s].astype(F32) + mine[...].astype(F32)).astype(BF16)
                    r_send(k, way, h, n, s + 1)

    def act_chunk(at, n):
        ob[:, pl.ds(at, n)] = jnp.dot(
            xs[...], wt[:, pl.ds(at, n)], preferred_element_type=F32
        ).astype(BF16)

    wait_bytes(xq.at[pl.ds(0, tok)], sq_sem.at[1, 0])
    wait_bytes(xq.at[pl.ds(0, tok)], load_sem.at[4])
    turn(0, early)
    x_own(0)
    w_arrive(0, (0, 1))
    x_forward(0)
    w_arrive(0, (2, 3))
    x_own(1)
    w_arrive(1, (0, 1))
    og_forward(0)
    x_complete(0)

    @pl.loop(0, NZ)
    def _(zb):
        send(
            xs.at[pl.ds(tok, tok), own_block(zb, 1 - c)],
            xq.at[pl.ds(3 * tok, tok), aligned(zb * 128, 128)],
            sq_sem.at[0, 1], sq_sem.at[1, 1], sister,
        )
        pltpu.make_async_copy(
            xs.at[pl.ds(tok, tok), own_block(zb, c)],
            xq.at[pl.ds(2 * tok, tok), aligned(zb * 128, 128)],
            load_sem.at[5],
        ).start()

    w_arrive(1, (2, 3))

    load_og.wait()
    og_own.wait_recv()
    wait_bytes(xq.at[pl.ds(0, tok)], sq_sem.at[1, 1])
    wait_bytes(xq.at[pl.ds(0, tok)], load_sem.at[5])
    turn(early, padded - early)
    w_arrive(2, (0, 1))
    og_arrive(0)
    pl.loop(0, wide // 256)(dw_chunk)
    r_send(0, 1, 0, 4, 0)
    r_send(3, -1, 0, 3, 0)
    x_forward(1)
    og_forward(1)
    w_arrive(2, (2, 3))
    og_arrive(1)
    pl.loop(wide // 256, cols // 256)(dw_chunk)
    r_send(1, -1, 1, 4, 0)
    r_send(2, 1, 1, 3, 0)
    w_arrive(3, (0, 1))

    wait_own(r1, b1r_sem)

    @pl.loop(0, NGROUP)
    def _(j):
        s2[j] = r1[inverse[j]]

    load_x.wait()
    x_complete(1)
    wait_bytes(wt.at[pl.ds(0, depth // 2)], sw_sem.at[1])
    act_chunk(0, 256)
    r_arrive(0, (0, 3))
    act_chunk(256, 256)
    act_chunk(512, 256)
    r_arrive(0, (1, 2))
    act_chunk(768, 128)
    their = send(
        ob.at[pl.ds(tok, tok)], act.at[:, aligned(yl * half, half)], ao_sem.at[0], ao_sem.at[1], y_near
    )
    own_act = pltpu.make_async_copy(
        ob.at[pl.ds(0, tok)], act.at[:, aligned(yl * half, half)], ao_sem.at[2]
    )
    own_act.start()
    r_arrive(1, (0, 3))
    r_arrive(1, (1, 2))
    r_arrive(2, (0, 3))
    r_arrive(2, (1, 2))

    def second_exchange(n):
        @pl.loop(0, NGROUP)
        def _(j):
            @pl.when(g != j)
            def _():
                send(
                    s2.at[j, :, pl.ds(0, n)], b2.at[g, :, pl.ds(0, n)],
                    b2s_sem, b2r_sem.at[0 if n == bw else 1], (j, l),
                )

        b2[g, :, pl.ds(0, n)] = s2[g, :, pl.ds(0, n)]

    by_width(second_exchange)

    r_arrive(3, (0, 1))
    load_m1.wait()
    load_m2.wait()

    @pl.loop(0, rows // bh)
    def _(q):
        at = aligned(q * bh, bh)
        for h, (up, down) in enumerate(((rp0.at[3], rm0.at[2]), (rp1.at[2], rm1.at[3]))):
            here = pl.ds(h * half, half)
            gradient = (
                dw[aligned(z * rows + q * bh, bh), here].astype(F32)
                + up[at, :].astype(F32) + down[at, :].astype(F32)
            )
            one = 0.9 * m1[at, here] + 0.1 * gradient
            two = 0.95 * m2[at, here] + 0.05 * gradient * gradient
            old = ms[at, here]
            new_1[at, here] = one
            new_2[at, here] = two
            new_ms[at, here] = old - 0.0003 * (one / (jnp.sqrt(two) + 1e-08) + 0.1 * old)

    wait_all(b2, b2r_sem)

    @pl.loop(0, NGROUP // 4)
    def _(q):
        for r in range(4):
            bk[aligned(q * bh, bh), pl.ds(bw * r, bwidth[r])] = (
                b2[4 * q + r, :, pl.ds(0, bwidth[r])].astype(F32)
            )

    wait_bytes(wt.at[pl.ds(0, 15 * wrows)], aw_sem.at[0])
    for copy in far + near + later + [og_own]:
        copy.wait_send()
    for n in range(2):
        wait_bytes(xq.at[pl.ds(0, tok)], sq_sem.at[0, n])
    wait_bytes(wt.at[pl.ds(0, depth // 2)], sw_sem.at[0])
    wait_all(r1, b1s_sem)
    wait_own(b2, b2s_sem)
    their.wait()
    own_act.wait()


def exchange(partner, inputs, weight, out_grad, master, moment_one, moment_two):
    tok, depth = inputs.shape
    cols = out_grad.shape[1]
    rows = master.shape[0]
    padded = -(-4 * tok // 256) * 256
    half = cols // 2
    dma = pltpu.SemaphoreType.DMA
    hbm = pl.BlockSpec(memory_space=pl.ANY)
    vmem = pl.BlockSpec(memory_space=pltpu.VMEM)
    return pl.pallas_call(
        kernel,
        out_shape=(pltpu.VMEM((tok, cols), BF16),) + (pltpu.VMEM((rows, cols), F32),) * 4,
        in_specs=[pl.BlockSpec(memory_space=pltpu.SMEM)] + [hbm] * 6,
        out_specs=(vmem,) * 5,
        scratch_shapes=[
            pltpu.VMEM((2 * tok, depth), BF16),
            pltpu.VMEM((depth, half), BF16),
            pltpu.VMEM((padded, NZ * rows), BF16),
            pltpu.VMEM((NZ * rows, padded), BF16),
            pltpu.VMEM((padded, cols), BF16),
            pltpu.VMEM((NZ * rows, cols), BF16),
            pltpu.VMEM((4, rows, half), BF16),
            pltpu.VMEM((3, rows, half), BF16),
            pltpu.VMEM((3, rows, half), BF16),
            pltpu.VMEM((4, rows, half), BF16),
            pltpu.VMEM((2 * tok, half), BF16),
            pltpu.VMEM((rows, cols), F32),
            pltpu.VMEM((rows, cols), F32),
            pltpu.VMEM((rows, cols), F32),
            pltpu.VMEM((rows, cols), BF16),
            pltpu.VMEM((NGROUP, rows // 8, 512), BF16),
            pltpu.VMEM((NGROUP, rows // 8, 512), BF16),
            pltpu.VMEM((NGROUP, rows // 8, 512), BF16),
            pltpu.SMEM((NGROUP,), jnp.int32),
            dma((8,)), dma((2,)), dma((2, 2)), dma((2, 6)), dma((2, 6)), dma((2, 2)), dma((2, 3)), dma((2, 2)),
            dma((4, 4)), dma((4, 4)), dma((2,)), dma((4, 4)), dma((4, 4)), dma((3,)), dma, dma((2,)), dma((2,)), dma,
        ],
        compiler_params=pltpu.CompilerParams(
            collective_id=0, has_side_effects=True, vmem_limit_bytes=50 * 2**20
        ),
    )(partner, inputs, weight, out_grad, master, moment_one, moment_two)


def store(*refs):
    count = len(refs) // 2
    copies = []
    for i in range(count):
        rows = refs[i].shape[0]
        cut = rows // 32 * 16
        for k, at in enumerate((pl.ds(0, cut), pl.ds(cut, rows - cut))):
            copies.append(pltpu.make_async_copy(refs[i].at[at], refs[count + i].at[at], refs[-1].at[i, k]))
    for copy in copies:
        copy.start()
    for copy in copies:
        copy.wait()


def on_device(inputs, weight, out_grad, master, moment_one, moment_two, partner):
    results = exchange(partner, inputs, weight, out_grad, master, moment_one, moment_two)
    return pl.pallas_call(
        store,
        out_shape=tuple(jax.ShapeDtypeStruct(r.shape, r.dtype) for r in results),
        in_specs=[pl.BlockSpec(memory_space=pl.ANY)] * len(results),
        out_specs=(pl.BlockSpec(memory_space=pl.ANY),) * len(results),
        scratch_shapes=[pltpu.SemaphoreType.DMA((len(results), 2))],
        compiler_params=pltpu.CompilerParams(vmem_limit_bytes=8 * 2**20),
    )(*results)


def solution(mesh):
    split = P("group", "local")
    return jax.shard_map(
        on_device,
        mesh=mesh,
        in_specs=(P("group", None), P(("group", "local"), None), split, split, split, split, P()),
        out_specs=(split,) * 5,
        check_vma=False,
    )
```
